256 devices in a mesh: wide: 64 (over z, y, x_hi), narrow: 4 (over x_lo, core).
Axes of the slice: x: 4 (x_hi: 2, x_lo: 2; x = x_hi * 2 + x_lo), y: 4, z: 8, core: 2. Of those that a mesh axis runs over, the one named last changes fastest.
Arguments:
- features: bfloat16 [65536, 2048], P(('wide', 'narrow')), may hold values from -6 to 6
- projection: bfloat16 [2048, 32], replicated, may hold values from -0.125 to 0.125
- targets: float32 [65536], P(('wide', 'narrow')), may hold values from -9 to 9
Outputs:
- solution: float32 [65536], P(('wide', 'narrow'))
- residual: float32 [65536], P(('wide', 'narrow'))
The draws below stay inside these ranges and needn't reach their ends.
All inputs are finite; a program needn't handle non-finite values.
Results may differ from the reference program's by a relative error of at most 0.0003.
Values sent between devices are 32-bit elements; how exact they have to be, the bound alone decides.
A program may use at most 64 MiB of HBM per device.

```python
import math
import jax
import jax.numpy as jnp
from jax import lax

FEAT = 2048
PROJ = 32
ITERS = 2
SOURCES = 65536


def draw_targets(key, part):
    key = jax.random.fold_in(key, 7)
    position = jnp.arange(SOURCES, dtype=jnp.float32) / SOURCES
    base = jnp.clip(jax.random.normal(key, (SOURCES,), jnp.float32), -5.0, 5.0)
    growth = jnp.exp(0.5 * jnp.log(3.0) * position)
    return base * growth


def block_scale(rng, shape, split, smallest, largest):
    level = 1.0
    for dim, shards_of in split:
        heights = jax.random.uniform(jax.random.fold_in(jax.random.fold_in(rng, 6), dim), (shards_of,), jnp.float32, smallest / len(split), largest / len(split))
        level = level * jnp.repeat(jnp.exp(heights), shape[dim] // shards_of).reshape((-1,) + (1,) * (len(shape) - 1 - dim))
    return level


def scatter_about(rng, dims, spread, bound, shards=(), kind=jnp.bfloat16):
    level = block_scale(rng, dims, shards, -0.22, 0.18) if shards else 1.0
    entries = jax.random.normal(rng, dims, jnp.float32) * spread * level
    return jnp.minimum(jnp.maximum(entries, -bound), bound).astype(kind)


def setup_inputs(seed: int = 0) -> dict:
    streams_of = jax.random.split(jax.random.key(seed), 4)
    features = scatter_about(streams_of[0], (SOURCES, FEAT), 1.0, 6.0, ((0, 256),))
    projection = scatter_about(streams_of[1], (FEAT, PROJ), FEAT ** -0.5, 0.125)
    targets = draw_targets(jax.random.fold_in(streams_of[3], 71), 0)
    return dict(features=features, projection=projection, targets=targets)


noise_var = 0.5
highest = lax.Precision.HIGHEST


def kernel_block(left, left_square, right, right_square):
    cross = jnp.dot(left, right.T, precision=highest)
    distance = left_square[:, None] + right_square[None, :] - 2.0 * cross
    return jnp.exp(distance * (-2.0 / left.shape[1]))


def apply_operator(latent, squares, vector):
    total = latent.shape[0]
    width = math.gcd(total, 1024)
    blocks = latent.reshape(total // width, width, latent.shape[1])
    block_squares = squares.reshape(total // width, width)

    def one_block(pair):
        tile = kernel_block(pair[0], pair[1], latent, squares)
        return jnp.dot(tile, vector, precision=highest)

    products = lax.map(one_block, (blocks, block_squares)).reshape(total)
    return products + noise_var * vector


def reference(features, projection, targets):
    latent = jnp.dot(features, projection, preferred_element_type=jnp.float32)
    squares = jnp.sum(latent * latent, axis=1)
    solution = jnp.zeros_like(targets)
    residual = targets
    direction = targets
    norm_now = jnp.sum(residual * residual)
    for step in range(ITERS):
        image = apply_operator(latent, squares, direction)
        alpha = norm_now / jnp.sum(direction * image)
        solution = solution + alpha * direction
        residual = residual - alpha * image
        norm_next = jnp.sum(residual * residual)
        direction = residual + (norm_next / norm_now) * direction
        norm_now = norm_next
    return solution, residual
```

```python
import functools
import math

import jax
import jax.numpy as jnp
from jax import lax
from jax.experimental import pallas as pl
from jax.experimental.pallas import tpu as pltpu
from jax.sharding import PartitionSpec as P

MESH = pl.DeviceIdType.MESH
F32 = jnp.float32
BF16 = jnp.bfloat16

SHIFTS = (0, 1, -2, 3, -4, 5, -6, 7, 8)
PLANE = ((0, 0), (0, 1), (0, 3), (1, 0), (3, 0), (1, 1), (1, 3), (3, 1),
         (3, 3), (0, 2), (2, 0), (1, 2), (3, 2), (2, 1), (2, 3), (2, 2))
NB = 16
NC = 9
BLK = 256
PROJ = 32
ROWS = NB * BLK
COLS = NC * BLK
DEEP = 256
CHUNK = 1024
GROUP = 768
LANES = 128
SCALE = math.sqrt(4.0 / PROJ * math.log2(math.e))
NOISE = 0.5
DIAG = 1.0 + NOISE


def place():
    w = lax.axis_index("wide")
    n = lax.axis_index("narrow")
    z = w // 8
    y = (w // 2) % 4
    x = (w % 2) * 2 + n // 2
    core = n % 2
    return z * 2 + core, y, x


def device(a, y, x):
    z = a // 2
    core = a % 2
    return ((z * 4 + y) * 2 + x // 2, (x % 2) * 2 + core)


def body(feat_hbm, proj_hbm, targ_ref, sol_ref, res_ref,
         feat, proj, lat_row, lat_col, t_row, t_col, o_row, o_col,
         side_a, side_b, wide_u, tiles, row_acc, col_acc,
         rp1, cp1, rr1, cr1, rp2, cp2, rr2, cr2,
         sc_out, sc_in, load_sem, lat_send, lat_rrecv, lat_crecv,
         small_send, small_recv, o_rrecv):
    a, y, x = place()

    def along_row(j, sign):
        dy, dx = PLANE[j]
        return device(a, (y + sign * dy + 4) % 4, (x + sign * dx + 4) % 4)

    def along_col(shift):
        return device((a + shift + 32) % 16, y, x)

    def send(src, dst, ssem, rsem, where):
        pltpu.make_async_remote_copy(
            src_ref=src, dst_ref=dst, send_sem=ssem, recv_sem=rsem,
            device_id=where, device_id_type=MESH).start()

    def settle(ref, sem):
        pltpu.make_async_copy(ref, ref, sem).wait()

    load_f = pltpu.make_async_copy(feat_hbm, feat, load_sem.at[0])
    load_p = pltpu.make_async_copy(proj_hbm, proj, load_sem.at[1])
    load_f.start()
    load_p.start()

    barrier = pltpu.get_barrier_semaphore()
    for j in range(1, NB):
        pl.semaphore_signal(barrier, inc=1, device_id=along_row(j, 1), device_id_type=MESH)
    for s in range(1, 16):
        pl.semaphore_signal(barrier, inc=1, device_id=along_col(s), device_id_type=MESH)
    t_row[0] = targ_ref[...]
    t_col[0] = targ_ref[...]
    pl.semaphore_wait(barrier, 30)

    for j in range(1, NB):
        send(targ_ref, t_row.at[j], small_send.at[0], small_recv.at[0], along_row(j, -1))
    for k in range(1, NC):
        send(targ_ref, t_col.at[k], small_send.at[1], small_recv.at[1], along_col(-SHIFTS[k]))

    load_p.wait()
    load_f.wait()
    latent = lax.dot_general(proj[...], feat[...], (((1,), (1,)), ((), ())),
                             preferred_element_type=F32)
    lat_row[0] = latent * SCALE
    for k in range(1, NB):
        send(lat_row.at[0], lat_row.at[k], lat_send.at[0], lat_rrecv.at[k], along_row(k, -1))
        if k < NC:
            send(lat_row.at[0], lat_col.at[k], lat_send.at[1], lat_crecv.at[k],
                 along_col(-SHIFTS[k]))

    settle(t_row.at[pl.ds(1, NB - 1)], small_recv.at[0])
    settle(t_col.at[pl.ds(1, NC - 1)], small_recv.at[1])

    def spread(values, j):
        for h in range(BLK // LANES):
            piece = values[:, h * LANES:(h + 1) * LANES]
            wide_u[j * BLK + h * LANES:j * BLK + (h + 1) * LANES, :] = jnp.transpose(
                jnp.broadcast_to(piece, (LANES, LANES)))

    for j in range(NB):
        spread(t_row[j], j)

    def split(v):
        h = v.astype(BF16)
        rest = v - h.astype(F32)
        m = rest.astype(BF16)
        l = (rest - m.astype(F32)).astype(BF16)
        return h, m, l

    line = lax.broadcasted_iota(jnp.int32, (16, BLK), 0)

    def parts(v):
        h, m, l = split(v)
        half = jnp.sum(v * v, axis=0, keepdims=True) * -0.5
        qh, qm, ql = (jnp.broadcast_to(q.astype(F32), (16, BLK)) for q in split(half))
        return h, m, l, qh, qm, ql

    def extra(qh, qm, ql, first):
        one = jnp.where((line >= 3 - first) & (line < 6 - first), 1.0, 0.0)
        e = jnp.where(line == first, qh, jnp.where(line == first + 1, qm,
                                                   jnp.where(line == first + 2, ql, one)))
        return e.astype(BF16)

    zeros = jnp.zeros((DEEP - 6 * PROJ - 16, BLK), BF16)

    def build_a(j):
        h, m, l, qh, qm, ql = parts(lat_row[j])
        stack = jnp.concatenate([h, h, m, m, h, l, extra(qh, qm, ql, 0), zeros], axis=0)
        side_a[j * BLK:(j + 1) * BLK, :] = jnp.transpose(stack)

    def build_b(k):
        h, m, l, qh, qm, ql = parts(lat_row[0] if k == 0 else lat_col[k])
        side_b[:, k * BLK:(k + 1) * BLK] = jnp.concatenate(
            [h, m, h, m, l, h, extra(qh, qm, ql, 3), zeros], axis=0)

    def fold_rows(r, out):
        for i in range(CHUNK // LANES):
            lo = r * CHUNK + i * LANES
            sums = jnp.sum(jnp.transpose(row_acc[lo:lo + LANES, :]), axis=0, keepdims=True)
            out[lo // BLK, :, (lo % BLK):(lo % BLK) + LANES] = sums

    def send_rows(r, out, into, sem):
        for j in range(4 * r, 4 * r + 4):
            if j:
                send(out.at[j], into.at[j], small_send.at[sem], small_recv.at[sem],
                     along_row(j, 1))

    def send_cols(ks, out, into, sem):
        for k in ks:
            if k:
                send(out.at[k], into.at[k], small_send.at[sem], small_recv.at[sem],
                     along_col(SHIFTS[k]))

    have_a, have_b = set(), set()

    def step(r, c):
        for j in range(4 * r, 4 * r + 4):
            if j not in have_a:
                have_a.add(j)
                if j:
                    settle(lat_row.at[j], lat_rrecv.at[j])
                build_a(j)
        for k in range(3 * c, 3 * c + 3):
            if k not in have_b:
                have_b.add(k)
                if k:
                    settle(lat_col.at[k], lat_crecv.at[k])
                build_b(k)
        rows = slice(r * CHUNK, (r + 1) * CHUNK)
        cols = slice(c * GROUP, (c + 1) * GROUP)
        power = jnp.dot(side_a[rows, :], side_b[:, cols], preferred_element_type=F32)
        p = jnp.exp2(power)
        tiles[rows, cols] = p
        u = wide_u[rows, :]
        total = None
        for i in range(GROUP // LANES):
            lane = c * GROUP + i * LANES
            k = lane // BLK
            piece = p[:, i * LANES:(i + 1) * LANES]
            down = jnp.sum((piece * u).reshape(CHUNK // 8, 8, LANES), axis=0)
            if r == 0:
                col_acc[:, lane:lane + LANES] = down
            else:
                col_acc[:, lane:lane + LANES] += down
            if k not in (0, NC - 1):
                v = t_col[k, :, (lane % BLK):(lane % BLK) + LANES]
                total = piece * v if total is None else total + piece * v
        if c == 0:
            row_acc[rows, :] = total
        else:
            row_acc[rows, :] += total

    def fold_cols(ks, out):
        for k in ks:
            out[k] = jnp.sum(col_acc[:, k * BLK:(k + 1) * BLK], axis=0, keepdims=True)

    order = ((0, 0), (1, 0), (0, 1), (1, 1), (2, 0), (2, 1), (0, 2), (1, 2), (2, 2),
             (3, 0), (3, 1), (3, 2))
    for r, c in order:
        step(r, c)
        if r == 3:
            fold_cols(range(3 * c, 3 * c + 3), cp1)
            send_cols(range(3 * c, 3 * c + 3), cp1, cr1, 3)
        if c == 2:
            fold_rows(r, rp1)
            send_rows(r, rp1, rr1, 2)

    def gathered(rp, rr, cp, cr, own):
        settle(rr.at[pl.ds(1, NB - 1)], small_recv.at[2 if own else 4])
        settle(cr.at[pl.ds(1, NC - 1)], small_recv.at[3 if own else 5])
        total = rp[0] + cp[0]
        for j in range(1, NB):
            total = total + rr[j]
        for k in range(1, NC):
            total = total + cr[k]
        return total

    t = targ_ref[...]
    off = gathered(rp1, rr1, cp1, cr1, True) - t
    o_row[0] = off
    o_col[0] = off
    for j in range(1, NB):
        send(o_row.at[0], o_row.at[j], small_send.at[6], o_rrecv.at[j // 4], along_row(j, -1))
        if j < NC:
            send(o_row.at[0], o_col.at[j], small_send.at[7], small_recv.at[7],
                 along_col(-SHIFTS[j]))

    def halves(v):
        return v[:, :LANES] + v[:, LANES:]

    def share_rows(slot, values, sem):
        for i, v in enumerate(values):
            sc_out[slot, :, i * LANES:(i + 1) * LANES] = halves(v)
        for j in range(1, NB):
            send(sc_out.at[slot], sc_in.at[slot, j], small_send.at[sem], small_recv.at[sem],
                 along_row(j, -1))

    def summed(slot, sem):
        settle(sc_in.at[slot, pl.ds(1, NB - 1)], small_recv.at[sem])
        total = sc_out[slot]
        for j in range(1, NB):
            total = total + sc_in[slot, j]
        return total

    def share_cols(slot, total, sem):
        sc_out[slot] = total
        for s in range(1, NB):
            send(sc_out.at[slot], sc_in.at[slot, s], small_send.at[sem], small_recv.at[sem],
                 along_col(-s))

    def scalars(total):
        return [jnp.sum(total[:, i * LANES:(i + 1) * LANES], axis=1, keepdims=True)
                for i in range(3)]

    share_rows(0, (t * t, t * off, off * off), 8)

    settle(o_col.at[pl.ds(1, NC - 1)], small_recv.at[7])
    lane_v = [jnp.broadcast_to(o_col[l * LANES // BLK, :, (l * LANES) % BLK:(l * LANES) % BLK + LANES],
                               (8, LANES)) for l in range(2, 16)]
    downs = tuple(jnp.zeros((8, LANES), F32) for _ in range(COLS // LANES))
    TAKE = 64
    for r in range(4):
        lo = max(4 * r, 1)
        settle(o_row.at[pl.ds(lo, 4 * r + 4 - lo)], o_rrecv.at[r])
        for j in range(4 * r, 4 * r + 4):
            spread(o_row[j], j)

        def some(i, downs):
            start = pl.multiple_of(r * CHUNK + i * TAKE, TAKE)
            downs = list(downs)
            for g in range(TAKE // 8):
                at = pl.ds(start + g * 8, 8)
                u = wide_u[at, :]
                total = None
                for l in range(COLS // LANES):
                    piece = tiles[at, l * LANES:(l + 1) * LANES]
                    downs[l] = downs[l] + piece * u
                    if 2 <= l < 16:
                        w = piece * lane_v[l - 2]
                        total = w if total is None else total + w
                row_acc[at, :] = total
            return tuple(downs)

        downs = lax.fori_loop(0, CHUNK // TAKE, some, downs)
        fold_rows(r, rp2)
        send_rows(r, rp2, rr2, 4)
        if r == 2:
            share_cols(1, summed(0, 8), 9)

    for k in range(NC):
        cp2[k] = jnp.concatenate([jnp.sum(downs[2 * k], axis=0, keepdims=True),
                                  jnp.sum(downs[2 * k + 1], axis=0, keepdims=True)], axis=1)
    send_cols(range(NC), cp2, cr2, 5)

    quad = jnp.zeros((1, BLK), F32)
    for j in range(NB):
        quad = quad + o_row[j] * rp2[j]
    for k in range(NC):
        quad = quad + o_col[k] * cp2[k]

    s0, s1, s2 = scalars(summed(1, 9))
    below = DIAG * s0 + s1
    alpha = s0 / below
    gamma = s1 / below
    resid = gamma * t - alpha * off
    share_rows(2, (resid * resid, resid * t, quad), 10)
    product = gathered(rp2, rr2, cp2, cr2, False) - off
    share_cols(3, summed(2, 10), 11)
    n1, cross, s3 = scalars(summed(3, 11))
    beta = n1 / s0
    both = gamma + beta
    length = n1 + 2.0 * beta * cross + beta * beta * s0
    energy = (DIAG * length + both * both * s1 - 2.0 * alpha * both * s2
              + alpha * alpha * (s3 - s2))
    step2 = n1 / energy
    direction = resid + beta * t
    image = DIAG * direction + both * off - alpha * product
    sol_ref[...] = alpha * t + step2 * direction
    res_ref[...] = resid - step2 * image

    settle(t_row.at[pl.ds(1, NB - 1)], small_send.at[0])
    settle(t_col.at[pl.ds(1, NC - 1)], small_send.at[1])
    settle(lat_row.at[pl.ds(1, NB - 1)], lat_send.at[0])
    settle(lat_col.at[pl.ds(1, NC - 1)], lat_send.at[1])
    settle(rr1.at[pl.ds(1, NB - 1)], small_send.at[2])
    settle(cr1.at[pl.ds(1, NC - 1)], small_send.at[3])
    settle(rr2.at[pl.ds(1, NB - 1)], small_send.at[4])
    settle(cr2.at[pl.ds(1, NC - 1)], small_send.at[5])
    settle(o_row.at[pl.ds(1, NB - 1)], small_send.at[6])
    settle(o_col.at[pl.ds(1, NC - 1)], small_send.at[7])
    for slot in range(4):
        settle(sc_in.at[slot, pl.ds(1, NB - 1)], small_send.at[8 + slot])


def on_device(features, projection, targets):
    vm = pl.BlockSpec(memory_space=pltpu.VMEM)
    hbm = pl.BlockSpec(memory_space=pl.ANY)
    flat = jax.ShapeDtypeStruct((1, BLK), F32)
    dma = pltpu.SemaphoreType.DMA
    sol, res = pl.pallas_call(
        body,
        out_shape=(flat, flat),
        in_specs=[hbm, hbm, vm],
        out_specs=(vm, vm),
        scratch_shapes=[
            pltpu.VMEM((BLK, 2048), BF16), pltpu.VMEM((PROJ, 2048), BF16),
            pltpu.VMEM((NB, PROJ, BLK), F32), pltpu.VMEM((NC, PROJ, BLK), F32),
            pltpu.VMEM((NB, 1, BLK), F32), pltpu.VMEM((NC, 1, BLK), F32),
            pltpu.VMEM((NB, 1, BLK), F32), pltpu.VMEM((NC, 1, BLK), F32),
            pltpu.VMEM((ROWS, DEEP), BF16), pltpu.VMEM((DEEP, COLS), BF16),
            pltpu.VMEM((ROWS, LANES), F32), pltpu.VMEM((ROWS, COLS), F32),
            pltpu.VMEM((ROWS, LANES), F32), pltpu.VMEM((8, COLS), F32),
            pltpu.VMEM((NB, 1, BLK), F32), pltpu.VMEM((NC, 1, BLK), F32),
            pltpu.VMEM((NB, 1, BLK), F32), pltpu.VMEM((NC, 1, BLK), F32),
            pltpu.VMEM((NB, 1, BLK), F32), pltpu.VMEM((NC, 1, BLK), F32),
            pltpu.VMEM((NB, 1, BLK), F32), pltpu.VMEM((NC, 1, BLK), F32),
            pltpu.VMEM((4, 1, 3 * LANES), F32), pltpu.VMEM((4, NB, 1, 3 * LANES), F32),
            dma((2,)), dma((2,)), dma((NB,)), dma((NC,)),
            dma((12,)), dma((12,)), dma((4,)),
        ],
        compiler_params=pltpu.CompilerParams(
            collective_id=0, has_side_effects=True, vmem_limit_bytes=60 * 2**20),
        name="conjugate",
    )(features, projection.T, targets.reshape(1, BLK))
    return sol.reshape(BLK), res.reshape(BLK)


def solution(mesh):
    in_specs = (P(("wide", "narrow"), None), P(), P(("wide", "narrow")))
    out_specs = (P(("wide", "narrow")), P(("wide", "narrow")))
    return jax.shard_map(
        on_device, mesh=mesh, in_specs=in_specs, out_specs=out_specs, check_vma=False)
```

```python
import functools
import math

import jax
import jax.numpy as jnp
from jax import lax
from jax.experimental import pallas as pl
from jax.experimental.pallas import tpu as pltpu
from jax.sharding import PartitionSpec as P

MESH = pl.DeviceIdType.MESH
F32 = jnp.float32
BF16 = jnp.bfloat16

SHIFTS = (0, 1, -2, 3, -4, 5, -6, 7, 8)
PLANE = ((0, 0), (0, 1), (0, 3), (1, 0), (3, 0), (1, 1), (1, 3), (3, 1),
         (3, 3), (0, 2), (2, 0), (1, 2), (3, 2), (2, 1), (2, 3), (2, 2))
NB = 16
NC = 9
BLK = 256
PROJ = 32
ROWS = NB * BLK
COLS = NC * BLK
DEEP = 256
CHUNK = 1024
GROUP = 768
LANES = 128
SCALE = math.sqrt(4.0 / PROJ * math.log2(math.e))
NOISE = 0.5
DIAG = 1.0 + NOISE


NEAREST_LAST = sorted(
    ((dy, dx, dc) for dy in range(4) for dx in range(4) for dc in range(2)),
    key=lambda d: (-min(d[0], 4 - d[0]) - min(d[1], 4 - d[1]), -d[2]))


def place():
    w = lax.axis_index("wide")
    n = lax.axis_index("narrow")
    z = w // 8
    y = (w // 2) % 4
    x = (w % 2) * 2 + n // 2
    core = n % 2
    return z * 2 + core, y, x


def device(a, y, x):
    z = a // 2
    core = a % 2
    return ((z * 4 + y) * 2 + x // 2, (x % 2) * 2 + core)


def body(feat_hbm, proj_hbm, targ_ref, out_ref,
         feat, proj, lat_row, lat_col, t_row, t_col, o_row, o_col,
         side_a, side_b, wide_u, tiles, row_acc, col_acc,
         rp1, cp1, rr1, cr1, rp2, cp2, rr2, cr2,
         sc_out, sc_in, load_sem, lat_send, lat_rrecv, lat_crecv,
         small_send, small_recv, t_rrecv, t_crecv, o_rrecv, o_crecv):
    a, y, x = place()

    def along_row(j, sign):
        dy, dx = PLANE[j]
        return device(a, (y + sign * dy + 4) % 4, (x + sign * dx + 4) % 4)

    def along_col(shift):
        return device((a + shift + 32) % 16, y, x)

    def send(src, dst, ssem, rsem, where):
        pltpu.make_async_remote_copy(
            src_ref=src, dst_ref=dst, send_sem=ssem, recv_sem=rsem,
            device_id=where, device_id_type=MESH).start()

    def settle(ref, sem):
        pltpu.make_async_copy(ref, ref, sem).wait()

    load_f = pltpu.make_async_copy(feat_hbm, feat, load_sem.at[0])
    load_p = pltpu.make_async_copy(proj_hbm, proj, load_sem.at[1])
    load_f.start()
    load_p.start()

    barrier = pltpu.get_barrier_semaphore()
    for j in range(1, NB):
        pl.semaphore_signal(barrier, inc=1, device_id=along_row(j, 1), device_id_type=MESH)
    for s in range(1, 16):
        pl.semaphore_signal(barrier, inc=1, device_id=along_col(s), device_id_type=MESH)
    t_row[0] = targ_ref[...]
    t_col[0] = targ_ref[...]
    def spread(values, j):
        for h in range(BLK // LANES):
            piece = values[:, h * LANES:(h + 1) * LANES]
            wide_u[j * BLK + h * LANES:j * BLK + (h + 1) * LANES, :] = jnp.transpose(
                jnp.broadcast_to(piece, (LANES, LANES)))

    def split(v):
        h = v.astype(BF16)
        rest = v - h.astype(F32)
        m = rest.astype(BF16)
        l = (rest - m.astype(F32)).astype(BF16)
        return h, m, l

    line = lax.broadcasted_iota(jnp.int32, (16, BLK), 0)

    def parts(v):
        h, m, l = split(v)
        half = jnp.sum(v * v, axis=0, keepdims=True) * -0.5
        qh, qm, ql = (jnp.broadcast_to(q.astype(F32), (16, BLK)) for q in split(half))
        return h, m, l, qh, qm, ql

    def extra(qh, qm, ql, first):
        one = jnp.where((line >= 3 - first) & (line < 6 - first), 1.0, 0.0)
        e = jnp.where(line == first, qh, jnp.where(line == first + 1, qm,
                                                   jnp.where(line == first + 2, ql, one)))
        return e.astype(BF16)

    zeros = jnp.zeros((DEEP - 6 * PROJ - 16, BLK), BF16)

    def build_a(j):
        h, m, l, qh, qm, ql = parts(lat_row[j])
        stack = jnp.concatenate([h, h, m, m, h, l, extra(qh, qm, ql, 0), zeros], axis=0)
        side_a[j * BLK:(j + 1) * BLK, :] = jnp.transpose(stack)

    def build_b(k):
        h, m, l, qh, qm, ql = parts(lat_row[0] if k == 0 else lat_col[k])
        side_b[:, k * BLK:(k + 1) * BLK] = jnp.concatenate(
            [h, m, h, m, l, h, extra(qh, qm, ql, 3), zeros], axis=0)

    load_p.wait()
    load_f.wait()
    latent = lax.dot_general(proj[...], feat[...], (((1,), (1,)), ((), ())),
                             preferred_element_type=F32)
    lat_row[0] = latent * SCALE
    build_a(0)
    build_b(0)
    spread(t_row[0], 0)
    pl.semaphore_wait(barrier, 30)

    for j in range(1, NB):
        send(targ_ref, t_row.at[j], small_send.at[0], t_rrecv.at[j // 4], along_row(j, -1))
        if j < NC:
            send(targ_ref, t_col.at[j], small_send.at[1], t_crecv.at[j // 3],
                 along_col(-SHIFTS[j]))
    for j in range(1, NC):
        send(lat_row.at[0], lat_col.at[j], lat_send.at[1], lat_crecv.at[j],
             along_col(-SHIFTS[j]))
    for j in range(1, NB):
        send(lat_row.at[0], lat_row.at[j], lat_send.at[0], lat_rrecv.at[j], along_row(j, -1))

    def fold_rows(r, out):
        for i in range(CHUNK // LANES):
            lo = r * CHUNK + i * LANES
            sums = jnp.sum(jnp.transpose(row_acc[lo:lo + LANES, :]), axis=0, keepdims=True)
            out[lo // BLK, :, (lo % BLK):(lo % BLK) + LANES] = sums

    def send_rows(r, out, into, sem):
        for j in range(4 * r, 4 * r + 4):
            if j:
                send(out.at[j], into.at[j], small_send.at[sem], small_recv.at[sem],
                     along_row(j, 1))

    def send_cols(ks, out, into, sem):
        for k in ks:
            if k:
                send(out.at[k], into.at[k], small_send.at[sem], small_recv.at[sem],
                     along_col(SHIFTS[k]))

    seen_r, seen_c = set(), set()

    def slots(i, width):
        return range(max(width * i, 1), width * i + width)

    def span(ref, i, width):
        near = slots(i, width)
        return ref.at[pl.ds(near[0], len(near))]

    def step(r, c):
        first_r, first_c = r not in seen_r, c not in seen_c
        seen_r.add(r)
        seen_c.add(c)
        if first_r:
            settle(span(t_row, r, 4), t_rrecv.at[r])
            for j in slots(r, 4):
                spread(t_row[j], j)
        if first_c:
            settle(span(t_col, c, 3), t_crecv.at[c])
            for k in slots(c, 3):
                settle(lat_col.at[k], lat_crecv.at[k])
                build_b(k)
        if first_r:
            for j in slots(r, 4):
                settle(lat_row.at[j], lat_rrecv.at[j])
                build_a(j)
        rows = slice(r * CHUNK, (r + 1) * CHUNK)
        cols = slice(c * GROUP, (c + 1) * GROUP)
        power = jnp.dot(side_a[rows, :], side_b[:, cols], preferred_element_type=F32)
        p = jnp.exp2(power)
        tiles[rows, cols] = p
        u = wide_u[rows, :]
        total = None
        for i in range(GROUP // LANES):
            lane = c * GROUP + i * LANES
            k = lane // BLK
            piece = p[:, i * LANES:(i + 1) * LANES]
            down = jnp.sum((piece * u).reshape(CHUNK // 8, 8, LANES), axis=0)
            if first_c:
                col_acc[:, lane:lane + LANES] = down
            else:
                col_acc[:, lane:lane + LANES] += down
            if k not in (0, NC - 1):
                v = t_col[k, :, (lane % BLK):(lane % BLK) + LANES]
                total = piece * v if total is None else total + piece * v
        if first_r:
            row_acc[rows, :] = total
        else:
            row_acc[rows, :] += total

    def fold_cols(ks, out):
        for k in ks:
            out[k] = jnp.sum(col_acc[:, k * BLK:(k + 1) * BLK], axis=0, keepdims=True)

    def finish(order, i):
        r, c = order[i]
        later = order[i + 1:]
        return (all(r != q for q, _ in later), all(c != q for _, q in later))

    order = ((0, 0), (1, 0), (2, 0), (3, 0), (0, 1), (1, 1), (2, 1), (3, 1), (0, 2), (1, 2), (2, 2), (3, 2))
    for i, (r, c) in enumerate(order):
        step(r, c)
        end_r, end_c = finish(order, i)
        if end_c:
            fold_cols(range(3 * c, 3 * c + 3), cp1)
            send_cols(range(3 * c, 3 * c + 3), cp1, cr1, 3)
        if end_r:
            fold_rows(r, rp1)
            send_rows(r, rp1, rr1, 2)

    def gathered(rp, rr, cp, cr, own):
        settle(rr.at[pl.ds(1, NB - 1)], small_recv.at[2 if own else 4])
        settle(cr.at[pl.ds(1, NC - 1)], small_recv.at[3 if own else 5])
        total = rp[0] + cp[0]
        for j in range(1, NB):
            total = total + rr[j]
        for k in range(1, NC):
            total = total + cr[k]
        return total

    t = targ_ref[...]
    off = gathered(rp1, rr1, cp1, cr1, True) - t
    def halves(v):
        return v[:, :LANES] + v[:, LANES:]

    o_row[0] = off
    o_col[0] = off
    for j in range(1, NB):
        send(o_row.at[0], o_row.at[j], small_send.at[6], o_rrecv.at[j // 4], along_row(j, -1))
        if j < NC:
            send(o_col.at[0], o_col.at[j], small_send.at[7], o_crecv.at[j // 3],
                 along_col(-SHIFTS[j]))

    lane = lax.broadcasted_iota(jnp.int32, (1, LANES), 1)
    z, core = a // 2, a % 2
    ys = [(y + d) % 4 for d in range(4)]
    xs = [(x + d) % 4 for d in range(4)]
    cores = [core, 1 - core]

    def share(slot, values):
        line = jnp.zeros((1, LANES), F32)
        for i, v in enumerate(values):
            line = jnp.where(lane == i, jnp.sum(v, axis=1, keepdims=True), line)
        sc_out[slot] = line

        def plane(q, last):
            far = 4 + (1 - 2 * (q % 2)) * ((q + 1) // 2)
            base = ((z + far) % 8) * 4
            for i, (dy, dx, dc) in enumerate(NEAREST_LAST):
                if last and (dy, dx, dc) == (0, 0, 0):
                    continue
                where = ((base + ys[dy]) * 2 + xs[dx] // 2, (xs[dx] % 2) * 2 + cores[dc])
                send(sc_out.at[slot], sc_in.at[slot, q * 32 + i], small_send.at[8 + slot],
                     small_recv.at[8 + slot], where)

        def one(q, carry):
            plane(q, False)
            return carry

        lax.fori_loop(0, 7, one, 0)
        plane(7, True)

    def shared(slot):
        settle(sc_in.at[slot, pl.ds(0, 255)], small_recv.at[8 + slot])
        sums = [sc_out[slot]] + [sc_in[slot, i] for i in range(255)]
        while len(sums) > 1:
            sums = [p + q for p, q in zip(sums[::2], sums[1::2])] + sums[len(sums) & ~1:]
        return [sums[0][:, i:i + 1] for i in range(3)]

    share(0, (t * t, t * off, off * off))

    for c in range(3):
        settle(span(o_col, c, 3), o_crecv.at[c])
    lane_v = [jnp.broadcast_to(o_col[l * LANES // BLK, :, (l * LANES) % BLK:(l * LANES) % BLK + LANES],
                               (8, LANES)) for l in range(2, 16)]
    downs = tuple(jnp.zeros((8, LANES), F32) for _ in range(COLS // LANES))
    TAKE = 64
    for r in range(4):
        settle(span(o_row, r, 4), o_rrecv.at[r])
        for j in range(4 * r, 4 * r + 4):
            spread(o_row[j], j)

        def some(i, downs):
            start = pl.multiple_of(r * CHUNK + i * TAKE, TAKE)
            downs = list(downs)
            for g in range(TAKE // 8):
                at = pl.ds(start + g * 8, 8)
                u = wide_u[at, :]
                total = None
                for l in range(COLS // LANES):
                    piece = tiles[at, l * LANES:(l + 1) * LANES]
                    downs[l] = downs[l] + piece * u
                    if 2 <= l < 16:
                        w = piece * lane_v[l - 2]
                        total = w if total is None else total + w
                row_acc[at, :] = total
            return tuple(downs)

        downs = lax.fori_loop(0, CHUNK // TAKE, some, downs)
        fold_rows(r, rp2)
        send_rows(r, rp2, rr2, 4)

    for k in range(NC):
        cp2[k] = jnp.concatenate([jnp.sum(downs[2 * k], axis=0, keepdims=True),
                                  jnp.sum(downs[2 * k + 1], axis=0, keepdims=True)], axis=1)
    send_cols(range(NC), cp2, cr2, 5)

    quad = jnp.zeros((1, BLK), F32)
    for j in range(NB):
        quad = quad + o_row[j] * rp2[j]
    for k in range(NC):
        quad = quad + o_col[k] * cp2[k]

    s0, s1, s2 = shared(0)
    below = DIAG * s0 + s1
    alpha = s0 / below
    gamma = s1 / below
    resid = gamma * t - alpha * off
    share(1, (resid * resid, resid * t, quad))
    product = gathered(rp2, rr2, cp2, cr2, False) - off
    n1, cross, s3 = shared(1)
    beta = n1 / s0
    both = gamma + beta
    length = n1 + 2.0 * beta * cross + beta * beta * s0
    energy = (DIAG * length + both * both * s1 - 2.0 * alpha * both * s2
              + alpha * alpha * (s3 - s2))
    step2 = n1 / energy
    direction = resid + beta * t
    image = DIAG * direction + both * off - alpha * product
    out_ref[0] = alpha * t
    out_ref[1] = step2 * direction
    out_ref[2] = resid
    out_ref[3] = step2 * image

    settle(t_row.at[pl.ds(1, NB - 1)], small_send.at[0])
    settle(t_col.at[pl.ds(1, NC - 1)], small_send.at[1])
    settle(lat_row.at[pl.ds(1, NB - 1)], lat_send.at[0])
    settle(lat_col.at[pl.ds(1, NC - 1)], lat_send.at[1])
    settle(rr1.at[pl.ds(1, NB - 1)], small_send.at[2])
    settle(cr1.at[pl.ds(1, NC - 1)], small_send.at[3])
    settle(rr2.at[pl.ds(1, NB - 1)], small_send.at[4])
    settle(cr2.at[pl.ds(1, NC - 1)], small_send.at[5])
    settle(o_row.at[pl.ds(1, NB - 1)], small_send.at[6])
    settle(o_col.at[pl.ds(1, NC - 1)], small_send.at[7])
    for slot in range(2):
        settle(sc_in.at[slot, pl.ds(0, 255)], small_send.at[8 + slot])


def on_device(features, projection, targets):
    vm = pl.BlockSpec(memory_space=pltpu.VMEM)
    hbm = pl.BlockSpec(memory_space=pl.ANY)
    dma = pltpu.SemaphoreType.DMA
    terms = pl.pallas_call(
        body,
        out_shape=jax.ShapeDtypeStruct((4, 1, BLK), F32),
        in_specs=[hbm, hbm, vm],
        out_specs=vm,
        scratch_shapes=[
            pltpu.VMEM((BLK, 2048), BF16), pltpu.VMEM((PROJ, 2048), BF16),
            pltpu.VMEM((NB, PROJ, BLK), F32), pltpu.VMEM((NC, PROJ, BLK), F32),
            pltpu.VMEM((NB, 1, BLK), F32), pltpu.VMEM((NC, 1, BLK), F32),
            pltpu.VMEM((NB, 1, BLK), F32), pltpu.VMEM((NC, 1, BLK), F32),
            pltpu.VMEM((ROWS, DEEP), BF16), pltpu.VMEM((DEEP, COLS), BF16),
            pltpu.VMEM((ROWS, LANES), F32), pltpu.VMEM((ROWS, COLS), F32),
            pltpu.VMEM((ROWS, LANES), F32), pltpu.VMEM((8, COLS), F32),
            pltpu.VMEM((NB, 1, BLK), F32), pltpu.VMEM((NC, 1, BLK), F32),
            pltpu.VMEM((NB, 1, BLK), F32), pltpu.VMEM((NC, 1, BLK), F32),
            pltpu.VMEM((NB, 1, BLK), F32), pltpu.VMEM((NC, 1, BLK), F32),
            pltpu.VMEM((NB, 1, BLK), F32), pltpu.VMEM((NC, 1, BLK), F32),
            pltpu.VMEM((2, 1, LANES), F32), pltpu.VMEM((2, 256, 1, LANES), F32),
            dma((2,)), dma((2,)), dma((NB,)), dma((NC,)),
            dma((10,)), dma((10,)), dma((4,)), dma((3,)), dma((4,)), dma((3,)),
        ],
        compiler_params=pltpu.CompilerParams(
            collective_id=0, has_side_effects=True, vmem_limit_bytes=60 * 2**20),
        name="conjugate",
    )(features, projection.T, targets.reshape(1, BLK))
    terms = terms.reshape(4, BLK)
    return terms[0] + terms[1], terms[2] - terms[3]


def solution(mesh):
    in_specs = (P(("wide", "narrow"), None), P(), P(("wide", "narrow")))
    out_specs = (P(("wide", "narrow")), P(("wide", "narrow")))
    return jax.shard_map(
        on_device, mesh=mesh, in_specs=in_specs, out_specs=out_specs, check_vma=False)
```

```python
import functools
import math

import jax
import jax.numpy as jnp
from jax import lax
from jax.experimental import pallas as pl
from jax.experimental.pallas import tpu as pltpu
from jax.sharding import PartitionSpec as P

MESH = pl.DeviceIdType.MESH
F32 = jnp.float32
BF16 = jnp.bfloat16

SHIFTS = (0, 1, -2, 3, -4, 5, -6, 7, 8)
PLANE = ((0, 0), (0, 1), (0, 3), (1, 0), (3, 0), (1, 1), (1, 3), (3, 1),
         (3, 3), (0, 2), (2, 0), (1, 2), (3, 2), (2, 1), (2, 3), (2, 2))
NB = 16
NC = 9
BLK = 256
PROJ = 32
ROWS = NB * BLK
COLS = NC * BLK
DEEP = 256
CHUNK = 1024
GROUP = 768
LANES = 128
SCALE = math.sqrt(4.0 / PROJ * math.log2(math.e))
NOISE = 0.5
DIAG = 1.0 + NOISE


NEAREST_LAST = sorted(
    ((dy, dx, dc) for dy in range(4) for dx in range(4) for dc in range(2)),
    key=lambda d: (-min(d[0], 4 - d[0]) - min(d[1], 4 - d[1]), -d[2]))


def place():
    w = lax.axis_index("wide")
    n = lax.axis_index("narrow")
    z = w // 8
    y = (w // 2) % 4
    x = (w % 2) * 2 + n // 2
    core = n % 2
    return z * 2 + core, y, x


def device(a, y, x):
    z = a // 2
    core = a % 2
    return ((z * 4 + y) * 2 + x // 2, (x % 2) * 2 + core)


def body(feat_hbm, proj_hbm, targ_ref, out_ref,
         feat, proj, lat_row, lat_col, t_row, t_col, o_row, o_col,
         side_a, side_b, wide_u, tiles, row_acc, col_acc,
         rp1, cp1, rr1, cr1, rp2, cp2, rr2, cr2,
         sc_out, sc_in, rs_in, cs_in, load_sem, lat_send, lat_rrecv, lat_crecv,
         small_send, small_recv, t_rrecv, t_crecv, o_rrecv, o_crecv):
    a, y, x = place()

    def along_row(j, sign):
        dy, dx = PLANE[j]
        return device(a, (y + sign * dy + 4) % 4, (x + sign * dx + 4) % 4)

    def along_col(shift):
        return device((a + shift + 32) % 16, y, x)

    def send(src, dst, ssem, rsem, where):
        pltpu.make_async_remote_copy(
            src_ref=src, dst_ref=dst, send_sem=ssem, recv_sem=rsem,
            device_id=where, device_id_type=MESH).start()

    def settle(ref, sem):
        pltpu.make_async_copy(ref, ref, sem).wait()

    load_f = pltpu.make_async_copy(feat_hbm, feat, load_sem.at[0])
    load_p = pltpu.make_async_copy(proj_hbm, proj, load_sem.at[1])
    load_f.start()
    load_p.start()

    barrier = pltpu.get_barrier_semaphore()
    for j in range(NB - 1, 0, -1):
        pl.semaphore_signal(barrier, inc=1, device_id=along_row(j, 1), device_id_type=MESH)
        if j < NC:
            pl.semaphore_signal(barrier, inc=1, device_id=along_col(SHIFTS[j]),
                                device_id_type=MESH)
    t_row[0] = targ_ref[...]
    t_col[0] = targ_ref[...]
    def spread(values, j):
        for h in range(BLK // LANES):
            piece = values[:, h * LANES:(h + 1) * LANES]
            wide_u[j * BLK + h * LANES:j * BLK + (h + 1) * LANES, :] = jnp.transpose(
                jnp.broadcast_to(piece, (LANES, LANES)))

    def split(v):
        h = v.astype(BF16)
        rest = v - h.astype(F32)
        m = rest.astype(BF16)
        l = (rest - m.astype(F32)).astype(BF16)
        return h, m, l

    line = lax.broadcasted_iota(jnp.int32, (16, BLK), 0)

    def parts(v):
        h, m, l = split(v)
        half = jnp.sum(v * v, axis=0, keepdims=True) * -0.5
        qh, qm, ql = (jnp.broadcast_to(q.astype(F32), (16, BLK)) for q in split(half))
        return h, m, l, qh, qm, ql

    def extra(qh, qm, ql, first):
        one = jnp.where((line >= 3 - first) & (line < 6 - first), 1.0, 0.0)
        e = jnp.where(line == first, qh, jnp.where(line == first + 1, qm,
                                                   jnp.where(line == first + 2, ql, one)))
        return e.astype(BF16)

    zeros = jnp.zeros((DEEP - 6 * PROJ - 16, BLK), BF16)

    def build_a(j):
        h, m, l, qh, qm, ql = parts(lat_row[j])
        stack = jnp.concatenate([h, h, m, m, h, l, extra(qh, qm, ql, 0), zeros], axis=0)
        side_a[j * BLK:(j + 1) * BLK, :] = jnp.transpose(stack)

    def build_b(k):
        h, m, l, qh, qm, ql = parts(lat_row[0] if k == 0 else lat_col[k])
        side_b[:, k * BLK:(k + 1) * BLK] = jnp.concatenate(
            [h, m, h, m, l, h, extra(qh, qm, ql, 3), zeros], axis=0)

    load_p.wait()
    load_f.wait()
    latent = lax.dot_general(proj[...], feat[...], (((1,), (1,)), ((), ())),
                             preferred_element_type=F32)
    lat_row[0] = latent * SCALE
    build_a(0)
    build_b(0)
    spread(t_row[0], 0)
    pl.semaphore_wait(barrier, NB + NC - 2)

    for j in range(1, NB):
        send(targ_ref, t_row.at[j], small_send.at[0], t_rrecv.at[j // 4], along_row(j, -1))
        if j < NC:
            send(targ_ref, t_col.at[j], small_send.at[1], t_crecv.at[j // 3],
                 along_col(-SHIFTS[j]))
    for j in range(1, NC):
        send(lat_row.at[0], lat_col.at[j], lat_send.at[1], lat_crecv.at[j],
             along_col(-SHIFTS[j]))
    for j in range(1, NB):
        send(lat_row.at[0], lat_row.at[j], lat_send.at[0], lat_rrecv.at[j], along_row(j, -1))

    def fold_rows(r, out):
        for i in range(CHUNK // LANES):
            lo = r * CHUNK + i * LANES
            sums = jnp.sum(jnp.transpose(row_acc[lo:lo + LANES, :]), axis=0, keepdims=True)
            out[lo // BLK, :, (lo % BLK):(lo % BLK) + LANES] = sums

    def send_rows(r, out, into, sem):
        for j in range(4 * r, 4 * r + 4):
            if j:
                send(out.at[j], into.at[j], small_send.at[sem], small_recv.at[sem],
                     along_row(j, 1))

    def send_cols(ks, out, into, sem):
        for k in ks:
            if k:
                send(out.at[k], into.at[k], small_send.at[sem], small_recv.at[sem],
                     along_col(SHIFTS[k]))

    seen_r, seen_c = set(), set()

    def slots(i, width):
        return range(max(width * i, 1), width * i + width)

    def span(ref, i, width):
        near = slots(i, width)
        return ref.at[pl.ds(near[0], len(near))]

    def step(low, high, c):
        fresh, first_c = [r for r in range(low, high) if r not in seen_r], c not in seen_c
        seen_r.update(fresh)
        seen_c.add(c)
        for r in fresh:
            settle(span(t_row, r, 4), t_rrecv.at[r])
            for j in slots(r, 4):
                spread(t_row[j], j)
        if first_c:
            settle(span(t_col, c, 3), t_crecv.at[c])
            for k in slots(c, 3):
                settle(lat_col.at[k], lat_crecv.at[k])
                build_b(k)
        for r in fresh:
            for j in slots(r, 4):
                settle(lat_row.at[j], lat_rrecv.at[j])
                build_a(j)
        rows = slice(low * CHUNK, high * CHUNK)
        cols = slice(c * GROUP, (c + 1) * GROUP)
        power = jnp.dot(side_a[rows, :], side_b[:, cols], preferred_element_type=F32)
        p = jnp.exp2(power)
        tiles[rows, cols] = p
        u = wide_u[rows, :]
        total = None
        for i in range(GROUP // LANES):
            lane = c * GROUP + i * LANES
            k = lane // BLK
            piece = p[:, i * LANES:(i + 1) * LANES]
            down = jnp.sum((piece * u).reshape((high - low) * CHUNK // 8, 8, LANES), axis=0)
            if first_c:
                col_acc[:, lane:lane + LANES] = down
            else:
                col_acc[:, lane:lane + LANES] += down
            if k not in (0, NC - 1):
                v = t_col[k, :, (lane % BLK):(lane % BLK) + LANES]
                total = piece * v if total is None else total + piece * v
        if fresh:
            row_acc[rows, :] = total
        else:
            row_acc[rows, :] += total

    def fold_cols(ks, out):
        for k in ks:
            out[k] = jnp.sum(col_acc[:, k * BLK:(k + 1) * BLK], axis=0, keepdims=True)

    order = ((0, 1, 0), (1, 2, 0), (2, 3, 0), (3, 4, 0), (0, 2, 1), (2, 4, 1), (2, 4, 2), (1, 2, 2), (0, 1, 2))
    for i, (low, high, c) in enumerate(order):
        step(low, high, c)
        later = order[i + 1:]
        if all(q != c for _, _, q in later):
            fold_cols(range(3 * c, 3 * c + 3), cp1)
            send_cols(range(3 * c, 3 * c + 3), cp1, cr1, 3)
        for r in range(low, high):
            if all(not l <= r < h for l, h, _ in later):
                fold_rows(r, rp1)
                send_rows(r, rp1, rr1, 2)

    def gathered(rp, rr, cp, cr, own):
        settle(rr.at[pl.ds(1, NB - 1)], small_recv.at[2 if own else 4])
        settle(cr.at[pl.ds(1, NC - 1)], small_recv.at[3 if own else 5])
        total = rp[0] + cp[0]
        for j in range(1, NB):
            total = total + rr[j]
        for k in range(1, NC):
            total = total + cr[k]
        return total

    t = targ_ref[...]
    off = gathered(rp1, rr1, cp1, cr1, True) - t
    def halves(v):
        return v[:, :LANES] + v[:, LANES:]

    o_row[0] = off
    o_col[0] = off
    for j in range(1, NB):
        send(o_row.at[0], o_row.at[j], small_send.at[6], o_rrecv.at[j // 4], along_row(j, -1))
        if j < NC:
            send(o_col.at[0], o_col.at[j], small_send.at[7], o_crecv.at[j // 5],
                 along_col(-SHIFTS[j]))

    lane = lax.broadcasted_iota(jnp.int32, (1, LANES), 1)
    z, core = a // 2, a % 2
    ys = [(y + d) % 4 for d in range(4)]
    xs = [(x + d) % 4 for d in range(4)]
    cores = [core, 1 - core]

    def across(v):
        return jnp.sum(v, axis=1, keepdims=True)

    def packed(values):
        line = jnp.zeros((1, LANES), F32)
        for i, v in enumerate(values):
            line = jnp.where(lane == i, v, line)
        return line

    def added(first, ref, many):
        sums = [first] + [ref[i] for i in range(many)]
        while len(sums) > 1:
            sums = [p + q for p, q in zip(sums[::2], sums[1::2])] + sums[len(sums) & ~1:]
        return sums[0]

    def share(values):
        sc_out[0] = packed(values)

        def plane(q, last):
            far = 4 + (1 - 2 * (q % 2)) * ((q + 1) // 2)
            base = ((z + far) % 8) * 4
            for i, (dy, dx, dc) in enumerate(NEAREST_LAST):
                if last and (dy, dx, dc) == (0, 0, 0):
                    continue
                where = ((base + ys[dy]) * 2 + xs[dx] // 2, (xs[dx] % 2) * 2 + cores[dc])
                send(sc_out.at[0], sc_in.at[q * 32 + i], small_send.at[8],
                     small_recv.at[8], where)

        def one(q, carry):
            plane(q, False)
            return carry

        lax.fori_loop(0, 7, one, 0)
        plane(7, True)

    def shared():
        settle(sc_in.at[pl.ds(0, 255)], small_recv.at[8])
        return added(sc_out[0], sc_in, 255)

    share((across(t * t), across(t * off), across(off * off)))

    TAKE = 64
    every = range(COLS // LANES)
    near, far = every[:10], every[10:]
    lane_v, downs = {}, {}

    def look(lanes):
        for l in lanes:
            downs[l] = jnp.zeros((8, LANES), F32)
            if 2 <= l < 16:
                lane_v[l] = jnp.broadcast_to(
                    o_col[l // 2, :, (l % 2) * LANES:(l % 2) * LANES + LANES], (8, LANES))

    def sweep(r, lanes, first):
        def some(i, carry):
            start = pl.multiple_of(r * CHUNK + i * TAKE, TAKE)
            carry = list(carry)
            for g in range(TAKE // 8):
                at = pl.ds(start + g * 8, 8)
                u = wide_u[at, :]
                total = None if first else row_acc[at, :]
                for n, l in enumerate(lanes):
                    piece = tiles[at, l * LANES:(l + 1) * LANES]
                    carry[n] = carry[n] + piece * u
                    if l in lane_v:
                        w = piece * lane_v[l]
                        total = w if total is None else total + w
                row_acc[at, :] = total
            return tuple(carry)

        done = lax.fori_loop(0, CHUNK // TAKE, some, tuple(downs[l] for l in lanes))
        downs.update(zip(lanes, done))

    def arrive(r):
        settle(span(o_row, r, 4), o_rrecv.at[r])
        for j in range(4 * r, 4 * r + 4):
            spread(o_row[j], j)

    quad = jnp.zeros((1, BLK), F32)

    def leave(r, quad):
        fold_rows(r, rp2)
        send_rows(r, rp2, rr2, 4)
        for j in range(4 * r, 4 * r + 4):
            quad = quad + o_row[j] * rp2[j]
        return quad

    settle(o_col.at[pl.ds(1, 4)], o_crecv.at[0])
    look(near)
    arrive(0)
    sweep(0, near, True)
    arrive(1)
    sweep(1, near, True)
    settle(o_col.at[pl.ds(5, 4)], o_crecv.at[1])
    look(far)
    sweep(0, far, False)
    quad = leave(0, quad)
    sweep(1, far, False)
    quad = leave(1, quad)
    arrive(2)
    sweep(2, every, True)
    quad = leave(2, quad)
    arrive(3)

    total = shared()
    s0, s1, s2 = (total[:, i:i + 1] for i in range(3))
    below = DIAG * s0 + s1
    alpha = s0 / below
    gamma = s1 / below
    resid = gamma * t - alpha * off
    norm_own, cross_own = across(resid * resid), across(resid * t)

    sweep(3, every, True)
    for k in range(NC):
        cp2[k] = jnp.concatenate([jnp.sum(downs[2 * k], axis=0, keepdims=True),
                                  jnp.sum(downs[2 * k + 1], axis=0, keepdims=True)], axis=1)
    send_cols(range(NC), cp2, cr2, 5)
    quad = leave(3, quad)
    for k in range(NC):
        quad = quad + o_col[k] * cp2[k]
    sc_out[1] = packed((norm_own, cross_own, across(quad)))
    for j in range(1, NB):
        send(sc_out.at[1], rs_in.at[j - 1], small_send.at[9], small_recv.at[9], along_row(j, -1))
    settle(t_row.at[pl.ds(1, NB - 1)], small_send.at[0])
    settle(t_col.at[pl.ds(1, NC - 1)], small_send.at[1])
    settle(lat_row.at[pl.ds(1, NB - 1)], lat_send.at[0])
    settle(lat_col.at[pl.ds(1, NC - 1)], lat_send.at[1])
    settle(rr1.at[pl.ds(1, NB - 1)], small_send.at[2])
    settle(cr1.at[pl.ds(1, NC - 1)], small_send.at[3])
    settle(rr2.at[pl.ds(1, NB - 1)], small_send.at[4])
    settle(cr2.at[pl.ds(1, NC - 1)], small_send.at[5])
    settle(o_row.at[pl.ds(1, NB - 1)], small_send.at[6])
    settle(o_col.at[pl.ds(1, NC - 1)], small_send.at[7])
    settle(sc_in.at[pl.ds(0, 255)], small_send.at[8])
    settle(rs_in, small_recv.at[9])
    sc_out[2] = added(sc_out[1], rs_in, NB - 1)
    for i in range(1, NB):
        send(sc_out.at[2], cs_in.at[i - 1], small_send.at[10], small_recv.at[10], along_col(-i))
    product = gathered(rp2, rr2, cp2, cr2, False) - off
    settle(rs_in, small_send.at[9])
    settle(cs_in, small_send.at[10])
    settle(cs_in, small_recv.at[10])
    total = added(sc_out[2], cs_in, NB - 1)
    n1, cross, s3 = (total[:, i:i + 1] for i in range(3))
    beta = n1 / s0
    both = gamma + beta
    length = n1 + 2.0 * beta * cross + beta * beta * s0
    energy = (DIAG * length + both * both * s1 - 2.0 * alpha * both * s2
              + alpha * alpha * (s3 - s2))
    step2 = n1 / energy
    direction = resid + beta * t
    image = DIAG * direction + both * off - alpha * product
    out_ref[0] = alpha * t
    out_ref[1] = step2 * direction
    out_ref[2] = resid
    out_ref[3] = step2 * image


def on_device(features, projection, targets):
    vm = pl.BlockSpec(memory_space=pltpu.VMEM)
    hbm = pl.BlockSpec(memory_space=pl.ANY)
    dma = pltpu.SemaphoreType.DMA
    terms = pl.pallas_call(
        body,
        out_shape=jax.ShapeDtypeStruct((4, 1, BLK), F32),
        in_specs=[hbm, hbm, vm],
        out_specs=vm,
        scratch_shapes=[
            pltpu.VMEM((BLK, 2048), BF16), pltpu.VMEM((PROJ, 2048), BF16),
            pltpu.VMEM((NB, PROJ, BLK), F32), pltpu.VMEM((NC, PROJ, BLK), F32),
            pltpu.VMEM((NB, 1, BLK), F32), pltpu.VMEM((NC, 1, BLK), F32),
            pltpu.VMEM((NB, 1, BLK), F32), pltpu.VMEM((NC, 1, BLK), F32),
            pltpu.VMEM((ROWS, DEEP), BF16), pltpu.VMEM((DEEP, COLS), BF16),
            pltpu.VMEM((ROWS, LANES), F32), pltpu.VMEM((ROWS, COLS), F32),
            pltpu.VMEM((ROWS, LANES), F32), pltpu.VMEM((8, COLS), F32),
            pltpu.VMEM((NB, 1, BLK), F32), pltpu.VMEM((NC, 1, BLK), F32),
            pltpu.VMEM((NB, 1, BLK), F32), pltpu.VMEM((NC, 1, BLK), F32),
            pltpu.VMEM((NB, 1, BLK), F32), pltpu.VMEM((NC, 1, BLK), F32),
            pltpu.VMEM((NB, 1, BLK), F32), pltpu.VMEM((NC, 1, BLK), F32),
            pltpu.VMEM((3, 1, LANES), F32), pltpu.VMEM((255, 1, LANES), F32),
            pltpu.VMEM((NB - 1, 1, LANES), F32), pltpu.VMEM((NB - 1, 1, LANES), F32),
            dma((2,)), dma((2,)), dma((NB,)), dma((NC,)),
            dma((11,)), dma((11,)), dma((4,)), dma((3,)), dma((4,)), dma((2,)),
        ],
        compiler_params=pltpu.CompilerParams(
            collective_id=0, has_side_effects=True, vmem_limit_bytes=60 * 2**20),
        name="conjugate",
    )(features, projection.T, targets.reshape(1, BLK))
    terms = terms.reshape(4, BLK)
    return terms[0] + terms[1], terms[2] - terms[3]


def solution(mesh):
    in_specs = (P(("wide", "narrow"), None), P(), P(("wide", "narrow")))
    out_specs = (P(("wide", "narrow")), P(("wide", "narrow")))
    return jax.shard_map(
        on_device, mesh=mesh, in_specs=in_specs, out_specs=out_specs, check_vma=False)
```

```python
import functools
import math

import jax
import jax.numpy as jnp
from jax import lax
from jax.experimental import pallas as pl
from jax.experimental.pallas import tpu as pltpu
from jax.sharding import PartitionSpec as P

MESH = pl.DeviceIdType.MESH
F32 = jnp.float32
BF16 = jnp.bfloat16

SHIFTS = (0, 1, -2, 3, -4, 5, -6, 7, 8)
PLANE = ((0, 0), (0, 1), (0, 3), (1, 0), (3, 0), (1, 1), (1, 3), (3, 1),
         (3, 3), (0, 2), (2, 0), (1, 2), (3, 2), (2, 1), (2, 3), (2, 2))
NB = 16
NC = 9
BLK = 256
PROJ = 32
ROWS = NB * BLK
COLS = NC * BLK
DEEP = 256
CHUNK = 1024
GROUP = 768
LANES = 128
SCALE = math.sqrt(4.0 / PROJ * math.log2(math.e))
NOISE = 0.5
DIAG = 1.0 + NOISE


NEAREST_LAST = sorted(
    ((dy, dx, dc) for dy in range(4) for dx in range(4) for dc in range(2)),
    key=lambda d: (-min(d[0], 4 - d[0]) - min(d[1], 4 - d[1]), -d[2]))


def place():
    w = lax.axis_index("wide")
    n = lax.axis_index("narrow")
    z = w // 8
    y = (w // 2) % 4
    x = (w % 2) * 2 + n // 2
    core = n % 2
    return z * 2 + core, y, x


def device(a, y, x):
    z = a // 2
    core = a % 2
    return ((z * 4 + y) * 2 + x // 2, (x % 2) * 2 + core)


def body(feat_hbm, proj_hbm, targ_ref, out_ref,
         feat, proj, lat_row, lat_col, t_row, t_col, o_row, o_col,
         side_a, side_b, wide_u, tiles, row_acc, col_acc,
         rp1, cp1, rr1, cr1, rp2, cp2, rr2, cr2,
         sc_out, sc_in, load_sem, lat_send, lat_rrecv, lat_crecv,
         small_send, small_recv, t_rrecv, t_crecv, o_rrecv, o_crecv):
    a, y, x = place()

    def along_row(j, sign):
        dy, dx = PLANE[j]
        return device(a, (y + sign * dy + 4) % 4, (x + sign * dx + 4) % 4)

    def along_col(shift):
        return device((a + shift + 32) % 16, y, x)

    def send(src, dst, ssem, rsem, where):
        pltpu.make_async_remote_copy(
            src_ref=src, dst_ref=dst, send_sem=ssem, recv_sem=rsem,
            device_id=where, device_id_type=MESH).start()

    def settle(ref, sem):
        pltpu.make_async_copy(ref, ref, sem).wait()

    load_f = pltpu.make_async_copy(feat_hbm, feat, load_sem.at[0])
    load_p = pltpu.make_async_copy(proj_hbm, proj, load_sem.at[1])
    load_f.start()
    load_p.start()

    barrier = pltpu.get_barrier_semaphore()
    for j in range(NB - 1, 0, -1):
        pl.semaphore_signal(barrier, inc=1, device_id=along_row(j, 1), device_id_type=MESH)
        if j < NC:
            pl.semaphore_signal(barrier, inc=1, device_id=along_col(SHIFTS[j]),
                                device_id_type=MESH)
    t_row[0] = targ_ref[...]
    t_col[0] = targ_ref[...]
    def spread(values, j):
        for h in range(BLK // LANES):
            piece = values[:, h * LANES:(h + 1) * LANES]
            wide_u[j * BLK + h * LANES:j * BLK + (h + 1) * LANES, :] = jnp.transpose(
                jnp.broadcast_to(piece, (LANES, LANES)))

    def split(v):
        h = v.astype(BF16)
        rest = v - h.astype(F32)
        m = rest.astype(BF16)
        l = (rest - m.astype(F32)).astype(BF16)
        return h, m, l

    line = lax.broadcasted_iota(jnp.int32, (16, BLK), 0)

    def parts(v):
        h, m, l = split(v)
        half = jnp.sum(v * v, axis=0, keepdims=True) * -0.5
        qh, qm, ql = (jnp.broadcast_to(q.astype(F32), (16, BLK)) for q in split(half))
        return h, m, l, qh, qm, ql

    def extra(qh, qm, ql, first):
        one = jnp.where((line >= 3 - first) & (line < 6 - first), 1.0, 0.0)
        e = jnp.where(line == first, qh, jnp.where(line == first + 1, qm,
                                                   jnp.where(line == first + 2, ql, one)))
        return e.astype(BF16)

    zeros = jnp.zeros((DEEP - 6 * PROJ - 16, BLK), BF16)

    def build_a(j):
        h, m, l, qh, qm, ql = parts(lat_row[j])
        stack = jnp.concatenate([h, h, m, m, h, l, extra(qh, qm, ql, 0), zeros], axis=0)
        side_a[j * BLK:(j + 1) * BLK, :] = jnp.transpose(stack)

    def build_b(k):
        h, m, l, qh, qm, ql = parts(lat_row[0] if k == 0 else lat_col[k])
        side_b[:, k * BLK:(k + 1) * BLK] = jnp.concatenate(
            [h, m, h, m, l, h, extra(qh, qm, ql, 3), zeros], axis=0)

    load_p.wait()
    load_f.wait()
    latent = lax.dot_general(proj[...], feat[...], (((1,), (1,)), ((), ())),
                             preferred_element_type=F32)
    lat_row[0] = latent * SCALE
    pl.semaphore_wait(barrier, NB + NC - 2)

    for j in range(1, NB):
        send(targ_ref, t_row.at[j], small_send.at[0], t_rrecv.at[j // 4], along_row(j, -1))
        if j < NC:
            send(targ_ref, t_col.at[j], small_send.at[1], t_crecv.at[j // 3],
                 along_col(-SHIFTS[j]))
    for j in range(1, NC):
        send(lat_row.at[0], lat_col.at[j], lat_send.at[1], lat_crecv.at[j],
             along_col(-SHIFTS[j]))
    for j in range(1, NB):
        send(lat_row.at[0], lat_row.at[j], lat_send.at[0], lat_rrecv.at[j], along_row(j, -1))

    build_a(0)
    build_b(0)
    spread(t_row[0], 0)

    def fold_rows(r, out):
        for i in range(CHUNK // LANES):
            lo = r * CHUNK + i * LANES
            sums = jnp.sum(jnp.transpose(row_acc[lo:lo + LANES, :]), axis=0, keepdims=True)
            out[lo // BLK, :, (lo % BLK):(lo % BLK) + LANES] = sums

    def send_rows(r, out, into, sem):
        for j in range(4 * r, 4 * r + 4):
            if j:
                send(out.at[j], into.at[j], small_send.at[sem], small_recv.at[sem],
                     along_row(j, 1))

    def send_cols(ks, out, into, sem):
        for k in ks:
            if k:
                send(out.at[k], into.at[k], small_send.at[sem], small_recv.at[sem],
                     along_col(SHIFTS[k]))

    seen_r, seen_c = set(), set()

    def slots(i, width):
        return range(max(width * i, 1), width * i + width)

    def span(ref, i, width):
        near = slots(i, width)
        return ref.at[pl.ds(near[0], len(near))]

    def step(low, high, c):
        fresh, first_c = [r for r in range(low, high) if r not in seen_r], c not in seen_c
        seen_r.update(fresh)
        seen_c.add(c)
        for r in fresh:
            settle(span(t_row, r, 4), t_rrecv.at[r])
            for j in slots(r, 4):
                spread(t_row[j], j)
        if first_c:
            settle(span(t_col, c, 3), t_crecv.at[c])
            for k in slots(c, 3):
                settle(lat_col.at[k], lat_crecv.at[k])
                build_b(k)
        for r in fresh:
            for j in slots(r, 4):
                settle(lat_row.at[j], lat_rrecv.at[j])
                build_a(j)
        rows = slice(low * CHUNK, high * CHUNK)
        cols = slice(c * GROUP, (c + 1) * GROUP)
        power = jnp.dot(side_a[rows, :], side_b[:, cols], preferred_element_type=F32)
        p = jnp.exp2(power)
        tiles[rows, cols] = p
        u = wide_u[rows, :]
        total = None
        for i in range(GROUP // LANES):
            lane = c * GROUP + i * LANES
            k = lane // BLK
            piece = p[:, i * LANES:(i + 1) * LANES]
            down = jnp.sum((piece * u).reshape((high - low) * CHUNK // 8, 8, LANES), axis=0)
            if first_c:
                col_acc[:, lane:lane + LANES] = down
            else:
                col_acc[:, lane:lane + LANES] += down
            if k not in (0, NC - 1):
                v = t_col[k, :, (lane % BLK):(lane % BLK) + LANES]
                total = piece * v if total is None else total + piece * v
        if fresh:
            row_acc[rows, :] = total
        else:
            row_acc[rows, :] += total

    def fold_cols(ks, out):
        for k in ks:
            out[k] = jnp.sum(col_acc[:, k * BLK:(k + 1) * BLK], axis=0, keepdims=True)

    order = ((0, 1, 0), (1, 2, 0), (2, 3, 0), (3, 4, 0), (0, 2, 1), (2, 4, 1), (2, 4, 2), (1, 2, 2), (0, 1, 2))
    for i, (low, high, c) in enumerate(order):
        step(low, high, c)
        later = order[i + 1:]
        if all(q != c for _, _, q in later):
            fold_cols(range(3 * c, 3 * c + 3), cp1)
            send_cols(range(3 * c, 3 * c + 3), cp1, cr1, 3)
        for r in range(low, high):
            if all(not l <= r < h for l, h, _ in later):
                fold_rows(r, rp1)
                send_rows(r, rp1, rr1, 2)

    def gathered(rp, rr, cp, cr, own):
        settle(rr.at[pl.ds(1, NB - 1)], small_recv.at[2 if own else 4])
        settle(cr.at[pl.ds(1, NC - 1)], small_recv.at[3 if own else 5])
        total = rp[0] + cp[0]
        for j in range(1, NB):
            total = total + rr[j]
        for k in range(1, NC):
            total = total + cr[k]
        return total

    t = targ_ref[...]
    off = gathered(rp1, rr1, cp1, cr1, True) - t
    def halves(v):
        return v[:, :LANES] + v[:, LANES:]

    o_row[0] = off
    o_col[0] = off
    for j in range(1, NB):
        send(o_row.at[0], o_row.at[j], small_send.at[6], o_rrecv.at[j // 4], along_row(j, -1))
        if j < NC:
            send(o_col.at[0], o_col.at[j], small_send.at[7], o_crecv.at[j // 5],
                 along_col(-SHIFTS[j]))

    lane = lax.broadcasted_iota(jnp.int32, (1, LANES), 1)
    z, core = a // 2, a % 2
    ys = [(y + d) % 4 for d in range(4)]
    xs = [(x + d) % 4 for d in range(4)]
    cores = [core, 1 - core]

    def across(v):
        return jnp.sum(v, axis=1, keepdims=True)

    def share(slot, values, between=None):
        line = jnp.zeros((1, LANES), F32)
        for i, v in enumerate(values):
            line = jnp.where(lane == i, v, line)
        sc_out[slot] = line

        def plane(q, last):
            far = 4 + (1 - 2 * (q % 2)) * ((q + 1) // 2)
            base = ((z + far) % 8) * 4
            for i, (dy, dx, dc) in enumerate(NEAREST_LAST):
                if last and (dy, dx, dc) == (0, 0, 0):
                    continue
                where = ((base + ys[dy]) * 2 + xs[dx] // 2, (xs[dx] % 2) * 2 + cores[dc])
                send(sc_out.at[slot], sc_in.at[slot, q * 32 + i], small_send.at[8 + slot],
                     small_recv.at[8 + slot], where)

        def one(q, carry):
            plane(q, False)
            return carry

        lax.fori_loop(0, 4, one, 0)
        if between is not None:
            between()
        lax.fori_loop(4, 7, one, 0)
        plane(7, True)

    def shared(slot):
        settle(sc_in.at[slot, pl.ds(0, 255)], small_recv.at[8 + slot])
        sums = [sc_out[slot]] + [sc_in[slot, i] for i in range(255)]
        while len(sums) > 1:
            sums = [p + q for p, q in zip(sums[::2], sums[1::2])] + sums[len(sums) & ~1:]
        return [sums[0][:, i:i + 1] for i in range(3)]

    share(0, (across(t * t), across(t * off), across(off * off)))

    TAKE = 64
    every = range(COLS // LANES)
    near, far = every[:10], every[10:]
    lane_v, downs = {}, {}

    def look(lanes):
        for l in lanes:
            downs[l] = jnp.zeros((8, LANES), F32)
            if 2 <= l < 16:
                lane_v[l] = jnp.broadcast_to(
                    o_col[l // 2, :, (l % 2) * LANES:(l % 2) * LANES + LANES], (8, LANES))

    def sweep(r, lanes, first):
        def some(i, carry):
            start = pl.multiple_of(r * CHUNK + i * TAKE, TAKE)
            carry = list(carry)
            for g in range(TAKE // 8):
                at = pl.ds(start + g * 8, 8)
                u = wide_u[at, :]
                total = None if first else row_acc[at, :]
                for n, l in enumerate(lanes):
                    piece = tiles[at, l * LANES:(l + 1) * LANES]
                    carry[n] = carry[n] + piece * u
                    if l in lane_v:
                        w = piece * lane_v[l]
                        total = w if total is None else total + w
                row_acc[at, :] = total
            return tuple(carry)

        done = lax.fori_loop(0, CHUNK // TAKE, some, tuple(downs[l] for l in lanes))
        downs.update(zip(lanes, done))

    def arrive(r):
        settle(span(o_row, r, 4), o_rrecv.at[r])
        for j in range(4 * r, 4 * r + 4):
            spread(o_row[j], j)

    quad = jnp.zeros((1, BLK), F32)

    def leave(r, quad):
        fold_rows(r, rp2)
        if r < 3:
            send_rows(r, rp2, rr2, 4)
        for j in range(4 * r, 4 * r + 4):
            quad = quad + o_row[j] * rp2[j]
        return quad

    settle(o_col.at[pl.ds(1, 4)], o_crecv.at[0])
    look(near)
    arrive(0)
    sweep(0, near, True)
    arrive(1)
    sweep(1, near, True)
    settle(o_col.at[pl.ds(5, 4)], o_crecv.at[1])
    look(far)
    sweep(0, far, False)
    quad = leave(0, quad)
    sweep(1, far, False)
    quad = leave(1, quad)
    arrive(2)
    sweep(2, every, True)
    quad = leave(2, quad)
    arrive(3)

    s0, s1, s2 = shared(0)
    below = DIAG * s0 + s1
    alpha = s0 / below
    gamma = s1 / below
    resid = gamma * t - alpha * off
    norm_own, cross_own = across(resid * resid), across(resid * t)

    sweep(3, every, True)
    for k in range(NC):
        cp2[k] = jnp.concatenate([jnp.sum(downs[2 * k], axis=0, keepdims=True),
                                  jnp.sum(downs[2 * k + 1], axis=0, keepdims=True)], axis=1)
    quad = leave(3, quad)
    for k in range(NC):
        quad = quad + o_col[k] * cp2[k]

    def last_parts():
        send_rows(3, rp2, rr2, 4)
        send_cols(range(NC), cp2, cr2, 5)

    share(1, (norm_own, cross_own, across(quad)), last_parts)
    product = gathered(rp2, rr2, cp2, cr2, False) - off
    settle(t_row.at[pl.ds(1, NB - 1)], small_send.at[0])
    settle(t_col.at[pl.ds(1, NC - 1)], small_send.at[1])
    settle(lat_row.at[pl.ds(1, NB - 1)], lat_send.at[0])
    settle(lat_col.at[pl.ds(1, NC - 1)], lat_send.at[1])
    settle(rr1.at[pl.ds(1, NB - 1)], small_send.at[2])
    settle(cr1.at[pl.ds(1, NC - 1)], small_send.at[3])
    settle(rr2.at[pl.ds(1, NB - 1)], small_send.at[4])
    settle(cr2.at[pl.ds(1, NC - 1)], small_send.at[5])
    settle(o_row.at[pl.ds(1, NB - 1)], small_send.at[6])
    settle(o_col.at[pl.ds(1, NC - 1)], small_send.at[7])
    for slot in range(2):
        settle(sc_in.at[slot, pl.ds(0, 255)], small_send.at[8 + slot])

    n1, cross, s3 = shared(1)
    beta = n1 / s0
    both = gamma + beta
    length = n1 + 2.0 * beta * cross + beta * beta * s0
    energy = (DIAG * length + both * both * s1 - 2.0 * alpha * both * s2
              + alpha * alpha * (s3 - s2))
    step2 = n1 / energy
    direction = resid + beta * t
    image = DIAG * direction + both * off - alpha * product
    out_ref[0] = alpha * t
    out_ref[1] = step2 * direction
    out_ref[2] = resid
    out_ref[3] = step2 * image


def on_device(features, projection, targets):
    vm = pl.BlockSpec(memory_space=pltpu.VMEM)
    hbm = pl.BlockSpec(memory_space=pl.ANY)
    dma = pltpu.SemaphoreType.DMA
    terms = pl.pallas_call(
        body,
        out_shape=jax.ShapeDtypeStruct((4, 1, BLK), F32),
        in_specs=[hbm, hbm, vm],
        out_specs=vm,
        scratch_shapes=[
            pltpu.VMEM((BLK, 2048), BF16), pltpu.VMEM((PROJ, 2048), BF16),
            pltpu.VMEM((NB, PROJ, BLK), F32), pltpu.VMEM((NC, PROJ, BLK), F32),
            pltpu.VMEM((NB, 1, BLK), F32), pltpu.VMEM((NC, 1, BLK), F32),
            pltpu.VMEM((NB, 1, BLK), F32), pltpu.VMEM((NC, 1, BLK), F32),
            pltpu.VMEM((ROWS, DEEP), BF16), pltpu.VMEM((DEEP, COLS), BF16),
            pltpu.VMEM((ROWS, LANES), F32), pltpu.VMEM((ROWS, COLS), F32),
            pltpu.VMEM((ROWS, LANES), F32), pltpu.VMEM((8, COLS), F32),
            pltpu.VMEM((NB, 1, BLK), F32), pltpu.VMEM((NC, 1, BLK), F32),
            pltpu.VMEM((NB, 1, BLK), F32), pltpu.VMEM((NC, 1, BLK), F32),
            pltpu.VMEM((NB, 1, BLK), F32), pltpu.VMEM((NC, 1, BLK), F32),
            pltpu.VMEM((NB, 1, BLK), F32), pltpu.VMEM((NC, 1, BLK), F32),
            pltpu.VMEM((2, 1, LANES), F32), pltpu.VMEM((2, 256, 1, LANES), F32),
            dma((2,)), dma((2,)), dma((NB,)), dma((NC,)),
            dma((10,)), dma((10,)), dma((4,)), dma((3,)), dma((4,)), dma((2,)),
        ],
        compiler_params=pltpu.CompilerParams(
            collective_id=0, has_side_effects=True, vmem_limit_bytes=60 * 2**20),
        name="conjugate",
    )(features, projection.T, targets.reshape(1, BLK))
    terms = terms.reshape(4, BLK)
    return terms[0] + terms[1], terms[2] - terms[3]


def solution(mesh):
    in_specs = (P(("wide", "narrow"), None), P(), P(("wide", "narrow")))
    out_specs = (P(("wide", "narrow")), P(("wide", "narrow")))
    return jax.shard_map(
        on_device, mesh=mesh, in_specs=in_specs, out_specs=out_specs, check_vma=False)
```

```python
import functools
import math

import jax
import jax.numpy as jnp
from jax import lax
from jax.experimental import pallas as pl
from jax.experimental.pallas import tpu as pltpu
from jax.sharding import PartitionSpec as P

MESH = pl.DeviceIdType.MESH
F32 = jnp.float32
BF16 = jnp.bfloat16

SHIFTS = (0, 1, -2, 3, -4, 5, -6, 7, 8)
PLANE = ((0, 0), (0, 1), (0, 3), (1, 0), (3, 0), (1, 1), (1, 3), (3, 1),
         (3, 3), (0, 2), (2, 0), (1, 2), (3, 2), (2, 1), (2, 3), (2, 2))
NB = 16
NC = 9
BLK = 256
PROJ = 32
ROWS = NB * BLK
COLS = NC * BLK
DEEP = 256
CHUNK = 1024
GROUP = 768
LANES = 128
SCALE = math.sqrt(4.0 / PROJ * math.log2(math.e))
NOISE = 0.5
DIAG = 1.0 + NOISE


NEAREST_LAST = sorted(
    ((dy, dx, dc) for dy in range(4) for dx in range(4) for dc in range(2)),
    key=lambda d: (-min(d[0], 4 - d[0]) - min(d[1], 4 - d[1]), -d[2]))


def place():
    w = lax.axis_index("wide")
    n = lax.axis_index("narrow")
    z = w // 8
    y = (w // 2) % 4
    x = (w % 2) * 2 + n // 2
    core = n % 2
    return z * 2 + core, y, x


def device(a, y, x):
    z = a // 2
    core = a % 2
    return ((z * 4 + y) * 2 + x // 2, (x % 2) * 2 + core)


def body(feat_hbm, proj_hbm, targ_ref, out_ref,
         feat, proj, lat_row, lat_col, t_row, t_col, o_row, o_col,
         side_a, side_b, wide_u, tiles, row_acc, col_acc,
         rp1, cp1, rr1, cr1, rp2, cp2, rr2, cr2,
         sc_out, sc_in, load_sem, lat_send, lat_rrecv, lat_crecv,
         small_send, small_recv, t_rrecv, t_crecv, o_rrecv, o_crecv):
    a, y, x = place()

    def along_row(j, sign):
        dy, dx = PLANE[j]
        return device(a, (y + sign * dy + 4) % 4, (x + sign * dx + 4) % 4)

    def along_col(shift):
        return device((a + shift + 32) % 16, y, x)

    def send(src, dst, ssem, rsem, where):
        pltpu.make_async_remote_copy(
            src_ref=src, dst_ref=dst, send_sem=ssem, recv_sem=rsem,
            device_id=where, device_id_type=MESH).start()

    def settle(ref, sem):
        pltpu.make_async_copy(ref, ref, sem).wait()

    load_f = pltpu.make_async_copy(feat_hbm, feat, load_sem.at[0])
    load_p = pltpu.make_async_copy(proj_hbm, proj, load_sem.at[1])
    load_f.start()
    load_p.start()

    barrier = pltpu.get_barrier_semaphore()
    for j in range(NB - 1, 0, -1):
        pl.semaphore_signal(barrier, inc=1, device_id=along_row(j, 1), device_id_type=MESH)
        if j < NC:
            pl.semaphore_signal(barrier, inc=1, device_id=along_col(SHIFTS[j]),
                                device_id_type=MESH)
    t_row[0] = targ_ref[...]
    t_col[0] = targ_ref[...]
    def spread(values, j):
        for h in range(BLK // LANES):
            piece = values[:, h * LANES:(h + 1) * LANES]
            wide_u[j * BLK + h * LANES:j * BLK + (h + 1) * LANES, :] = jnp.transpose(
                jnp.broadcast_to(piece, (LANES, LANES)))

    def split(v):
        h = v.astype(BF16)
        rest = v - h.astype(F32)
        m = rest.astype(BF16)
        l = (rest - m.astype(F32)).astype(BF16)
        return h, m, l

    line = lax.broadcasted_iota(jnp.int32, (16, BLK), 0)

    def parts(v):
        h, m, l = split(v)
        half = jnp.sum(v * v, axis=0, keepdims=True) * -0.5
        qh, qm, ql = (jnp.broadcast_to(q.astype(F32), (16, BLK)) for q in split(half))
        return h, m, l, qh, qm, ql

    def extra(qh, qm, ql, first):
        one = jnp.where((line >= 3 - first) & (line < 6 - first), 1.0, 0.0)
        e = jnp.where(line == first, qh, jnp.where(line == first + 1, qm,
                                                   jnp.where(line == first + 2, ql, one)))
        return e.astype(BF16)

    zeros = jnp.zeros((DEEP - 6 * PROJ - 16, BLK), BF16)

    def build_a(j):
        h, m, l, qh, qm, ql = parts(lat_row[j])
        stack = jnp.concatenate([h, h, m, m, h, l, extra(qh, qm, ql, 0), zeros], axis=0)
        side_a[j * BLK:(j + 1) * BLK, :] = jnp.transpose(stack)

    def build_b(k):
        h, m, l, qh, qm, ql = parts(lat_row[0] if k == 0 else lat_col[k])
        side_b[:, k * BLK:(k + 1) * BLK] = jnp.concatenate(
            [h, m, h, m, l, h, extra(qh, qm, ql, 3), zeros], axis=0)

    load_p.wait()
    load_f.wait()
    latent = lax.dot_general(proj[...], feat[...], (((1,), (1,)), ((), ())),
                             preferred_element_type=F32)
    lat_row[0] = latent * SCALE
    pl.semaphore_wait(barrier, NB + NC - 2)

    for j in range(1, NB):
        send(targ_ref, t_row.at[j], small_send.at[0], t_rrecv.at[j // 4], along_row(j, -1))
        if j < NC:
            send(targ_ref, t_col.at[j], small_send.at[1], t_crecv.at[j // 3],
                 along_col(-SHIFTS[j]))
    for j in range(1, NC):
        send(lat_row.at[0], lat_col.at[j], lat_send.at[1], lat_crecv.at[j],
             along_col(-SHIFTS[j]))
    for j in range(1, NB):
        send(lat_row.at[0], lat_row.at[j], lat_send.at[0], lat_rrecv.at[j], along_row(j, -1))

    build_a(0)
    build_b(0)
    spread(t_row[0], 0)

    def fold_rows(r, out):
        for i in range(CHUNK // LANES):
            lo = r * CHUNK + i * LANES
            sums = jnp.sum(jnp.transpose(row_acc[lo:lo + LANES, :]), axis=0, keepdims=True)
            out[lo // BLK, :, (lo % BLK):(lo % BLK) + LANES] = sums

    def send_rows(r, out, into, sem):
        for j in range(4 * r, 4 * r + 4):
            if j:
                send(out.at[j], into.at[j], small_send.at[sem], small_recv.at[sem],
                     along_row(j, 1))

    def send_cols(ks, out, into, sem):
        for k in ks:
            if k:
                send(out.at[k], into.at[k], small_send.at[sem], small_recv.at[sem],
                     along_col(SHIFTS[k]))

    told, ready_r, ready_c = set(), {0}, {0}
    begun_r, begun_c = set(), set()

    def slots(i, width):
        return range(max(width * i, 1), width * i + width)

    def span(ref, i, width):
        near = slots(i, width)
        return ref.at[pl.ds(near[0], len(near))]

    def step(low, high, left, right):
        for j in range(low, high):
            if ("r", j // 4) not in told:
                told.add(("r", j // 4))
                settle(span(t_row, j // 4, 4), t_rrecv.at[j // 4])
        for k in range(left, right):
            if ("c", k // 3) not in told:
                told.add(("c", k // 3))
                settle(span(t_col, k // 3, 3), t_crecv.at[k // 3])
        for j in range(low, high):
            if j not in ready_r:
                spread(t_row[j], j)
        for k in range(left, right):
            if k not in ready_c:
                ready_c.add(k)
                settle(lat_col.at[k], lat_crecv.at[k])
                build_b(k)
        for j in range(low, high):
            if j not in ready_r:
                ready_r.add(j)
                settle(lat_row.at[j], lat_rrecv.at[j])
                build_a(j)
        rows = slice(low * BLK, high * BLK)
        cols = slice(left * BLK, right * BLK)
        power = jnp.dot(side_a[rows, :], side_b[:, cols], preferred_element_type=F32)
        p = jnp.exp2(power)
        tiles[rows, cols] = p
        u = wide_u[rows, :]
        total = None
        for i in range((right - left) * BLK // LANES):
            lane = left * BLK + i * LANES
            k = lane // BLK
            piece = p[:, i * LANES:(i + 1) * LANES]
            down = jnp.sum((piece * u).reshape((high - low) * BLK // 8, 8, LANES), axis=0)
            if k not in begun_c:
                col_acc[:, lane:lane + LANES] = down
            else:
                col_acc[:, lane:lane + LANES] += down
            if k not in (0, NC - 1):
                v = t_col[k, :, (lane % BLK):(lane % BLK) + LANES]
                total = piece * v if total is None else total + piece * v
        begun_c.update(range(left, right))
        if total is not None:
            if low in begun_r:
                row_acc[rows, :] += total
            else:
                row_acc[rows, :] = total
            begun_r.update(range(low, high))

    def fold_cols(ks, out):
        for k in ks:
            out[k] = jnp.sum(col_acc[:, k * BLK:(k + 1) * BLK], axis=0, keepdims=True)

    order = ((0, 4, 0, 3), (4, 8, 0, 3), (8, 12, 0, 3), (12, 14, 0, 3), (0, 4, 3, 6), (4, 8, 3, 6), (8, 14, 3, 6),
             (0, 8, 6, 9), (8, 14, 6, 9), (14, 16, 0, 9))
    sent_r = set()
    for i, (low, high, left, right) in enumerate(order):
        step(low, high, left, right)
        later = order[i + 1:]
        for k in range(left, right):
            if all(not l <= k < h for _, _, l, h in later):
                fold_cols([k], cp1)
                send_cols([k], cp1, cr1, 3)
        rest = [(b, e) for b, e, l, _ in later if l < NC - 1]
        for r in range(4):
            if r not in sent_r and all(e <= 4 * r or 4 * r + 4 <= b for b, e in rest):
                sent_r.add(r)
                fold_rows(r, rp1)
                send_rows(r, rp1, rr1, 2)

    def gathered(rp, rr, cp, cr, own):
        settle(rr.at[pl.ds(1, NB - 1)], small_recv.at[2 if own else 4])
        settle(cr.at[pl.ds(1, NC - 1)], small_recv.at[3 if own else 5])
        total = rp[0] + cp[0]
        for j in range(1, NB):
            total = total + rr[j]
        for k in range(1, NC):
            total = total + cr[k]
        return total

    t = targ_ref[...]
    off = gathered(rp1, rr1, cp1, cr1, True) - t
    def halves(v):
        return v[:, :LANES] + v[:, LANES:]

    o_row[0] = off
    o_col[0] = off
    for j in range(1, NB):
        send(o_row.at[0], o_row.at[j], small_send.at[6], o_rrecv.at[j // 4], along_row(j, -1))
        if j < NC:
            send(o_col.at[0], o_col.at[j], small_send.at[7], o_crecv.at[j // 5],
                 along_col(-SHIFTS[j]))

    lane = lax.broadcasted_iota(jnp.int32, (1, LANES), 1)
    z, core = a // 2, a % 2
    ys = [(y + d) % 4 for d in range(4)]
    xs = [(x + d) % 4 for d in range(4)]
    cores = [core, 1 - core]

    def across(v):
        return jnp.sum(v, axis=1, keepdims=True)

    def share(slot, values, between=None):
        line = jnp.zeros((1, LANES), F32)
        for i, v in enumerate(values):
            line = jnp.where(lane == i, v, line)
        sc_out[slot] = line

        def plane(q, last):
            far = 4 + (1 - 2 * (q % 2)) * ((q + 1) // 2)
            base = ((z + far) % 8) * 4
            for i, (dy, dx, dc) in enumerate(NEAREST_LAST):
                if last and (dy, dx, dc) == (0, 0, 0):
                    continue
                where = ((base + ys[dy]) * 2 + xs[dx] // 2, (xs[dx] % 2) * 2 + cores[dc])
                send(sc_out.at[slot], sc_in.at[slot, q * 32 + i], small_send.at[8 + slot],
                     small_recv.at[8 + slot], where)

        def one(q, carry):
            plane(q, False)
            return carry

        lax.fori_loop(0, 4, one, 0)
        if between is not None:
            between()
        lax.fori_loop(4, 7, one, 0)
        plane(7, True)

    def shared(slot):
        settle(sc_in.at[slot, pl.ds(0, 255)], small_recv.at[8 + slot])
        sums = [sc_out[slot]] + [sc_in[slot, i] for i in range(255)]
        while len(sums) > 1:
            sums = [p + q for p, q in zip(sums[::2], sums[1::2])] + sums[len(sums) & ~1:]
        return [sums[0][:, i:i + 1] for i in range(3)]

    share(0, (across(t * t), across(t * off), across(off * off)))

    TAKE = 64
    every = range(COLS // LANES)
    near, far = every[:10], every[10:]
    lane_v, downs = {}, {}

    def look(lanes):
        for l in lanes:
            downs[l] = jnp.zeros((8, LANES), F32)
            if 2 <= l < 16:
                lane_v[l] = jnp.broadcast_to(
                    o_col[l // 2, :, (l % 2) * LANES:(l % 2) * LANES + LANES], (8, LANES))

    def sweep(r, lanes, first):
        def some(i, carry):
            start = pl.multiple_of(r * CHUNK + i * TAKE, TAKE)
            carry = list(carry)
            for g in range(TAKE // 8):
                at = pl.ds(start + g * 8, 8)
                u = wide_u[at, :]
                total = None if first else row_acc[at, :]
                for n, l in enumerate(lanes):
                    piece = tiles[at, l * LANES:(l + 1) * LANES]
                    carry[n] = carry[n] + piece * u
                    if l in lane_v:
                        w = piece * lane_v[l]
                        total = w if total is None else total + w
                row_acc[at, :] = total
            return tuple(carry)

        done = lax.fori_loop(0, CHUNK // TAKE, some, tuple(downs[l] for l in lanes))
        downs.update(zip(lanes, done))

    def arrive(r):
        settle(span(o_row, r, 4), o_rrecv.at[r])
        for j in range(4 * r, 4 * r + 4):
            spread(o_row[j], j)

    quad = jnp.zeros((1, BLK), F32)

    def leave(r, quad):
        fold_rows(r, rp2)
        if r < 3:
            send_rows(r, rp2, rr2, 4)
        for j in range(4 * r, 4 * r + 4):
            quad = quad + o_row[j] * rp2[j]
        return quad

    settle(o_col.at[pl.ds(1, 4)], o_crecv.at[0])
    look(near)
    arrive(0)
    sweep(0, near, True)
    arrive(1)
    sweep(1, near, True)
    settle(o_col.at[pl.ds(5, 4)], o_crecv.at[1])
    look(far)
    sweep(0, far, False)
    quad = leave(0, quad)
    sweep(1, far, False)
    quad = leave(1, quad)
    arrive(2)
    sweep(2, every, True)
    quad = leave(2, quad)
    arrive(3)

    s0, s1, s2 = shared(0)
    below = DIAG * s0 + s1
    alpha = s0 / below
    gamma = s1 / below
    resid = gamma * t - alpha * off
    norm_own, cross_own = across(resid * resid), across(resid * t)

    sweep(3, every, True)
    for k in range(NC):
        cp2[k] = jnp.concatenate([jnp.sum(downs[2 * k], axis=0, keepdims=True),
                                  jnp.sum(downs[2 * k + 1], axis=0, keepdims=True)], axis=1)
    quad = leave(3, quad)
    for k in range(NC):
        quad = quad + o_col[k] * cp2[k]

    def last_parts():
        send_rows(3, rp2, rr2, 4)
        send_cols(range(NC), cp2, cr2, 5)

    share(1, (norm_own, cross_own, across(quad)), last_parts)
    product = gathered(rp2, rr2, cp2, cr2, False) - off
    settle(t_row.at[pl.ds(1, NB - 1)], small_send.at[0])
    settle(t_col.at[pl.ds(1, NC - 1)], small_send.at[1])
    settle(lat_row.at[pl.ds(1, NB - 1)], lat_send.at[0])
    settle(lat_col.at[pl.ds(1, NC - 1)], lat_send.at[1])
    settle(rr1.at[pl.ds(1, NB - 1)], small_send.at[2])
    settle(cr1.at[pl.ds(1, NC - 1)], small_send.at[3])
    settle(rr2.at[pl.ds(1, NB - 1)], small_send.at[4])
    settle(cr2.at[pl.ds(1, NC - 1)], small_send.at[5])
    settle(o_row.at[pl.ds(1, NB - 1)], small_send.at[6])
    settle(o_col.at[pl.ds(1, NC - 1)], small_send.at[7])
    for slot in range(2):
        settle(sc_in.at[slot, pl.ds(0, 255)], small_send.at[8 + slot])

    n1, cross, s3 = shared(1)
    beta = n1 / s0
    both = gamma + beta
    length = n1 + 2.0 * beta * cross + beta * beta * s0
    energy = (DIAG * length + both * both * s1 - 2.0 * alpha * both * s2
              + alpha * alpha * (s3 - s2))
    step2 = n1 / energy
    direction = resid + beta * t
    image = DIAG * direction + both * off - alpha * product
    out_ref[0] = alpha * t
    out_ref[1] = step2 * direction
    out_ref[2] = resid
    out_ref[3] = step2 * image


def on_device(features, projection, targets):
    vm = pl.BlockSpec(memory_space=pltpu.VMEM)
    hbm = pl.BlockSpec(memory_space=pl.ANY)
    dma = pltpu.SemaphoreType.DMA
    terms = pl.pallas_call(
        body,
        out_shape=jax.ShapeDtypeStruct((4, 1, BLK), F32),
        in_specs=[hbm, hbm, vm],
        out_specs=vm,
        scratch_shapes=[
            pltpu.VMEM((BLK, 2048), BF16), pltpu.VMEM((PROJ, 2048), BF16),
            pltpu.VMEM((NB, PROJ, BLK), F32), pltpu.VMEM((NC, PROJ, BLK), F32),
            pltpu.VMEM((NB, 1, BLK), F32), pltpu.VMEM((NC, 1, BLK), F32),
            pltpu.VMEM((NB, 1, BLK), F32), pltpu.VMEM((NC, 1, BLK), F32),
            pltpu.VMEM((ROWS, DEEP), BF16), pltpu.VMEM((DEEP, COLS), BF16),
            pltpu.VMEM((ROWS, LANES), F32), pltpu.VMEM((ROWS, COLS), F32),
            pltpu.VMEM((ROWS, LANES), F32), pltpu.VMEM((8, COLS), F32),
            pltpu.VMEM((NB, 1, BLK), F32), pltpu.VMEM((NC, 1, BLK), F32),
            pltpu.VMEM((NB, 1, BLK), F32), pltpu.VMEM((NC, 1, BLK), F32),
            pltpu.VMEM((NB, 1, BLK), F32), pltpu.VMEM((NC, 1, BLK), F32),
            pltpu.VMEM((NB, 1, BLK), F32), pltpu.VMEM((NC, 1, BLK), F32),
            pltpu.VMEM((2, 1, LANES), F32), pltpu.VMEM((2, 256, 1, LANES), F32),
            dma((2,)), dma((2,)), dma((NB,)), dma((NC,)),
            dma((10,)), dma((10,)), dma((4,)), dma((3,)), dma((4,)), dma((2,)),
        ],
        compiler_params=pltpu.CompilerParams(
            collective_id=0, has_side_effects=True, vmem_limit_bytes=60 * 2**20),
        name="conjugate",
    )(features, projection.T, targets.reshape(1, BLK))
    terms = terms.reshape(4, BLK)
    return terms[0] + terms[1], terms[2] - terms[3]


def solution(mesh):
    in_specs = (P(("wide", "narrow"), None), P(), P(("wide", "narrow")))
    out_specs = (P(("wide", "narrow")), P(("wide", "narrow")))
    return jax.shard_map(
        on_device, mesh=mesh, in_specs=in_specs, out_specs=out_specs, check_vma=False)
```

```python
import functools
import math

import jax
import jax.numpy as jnp
from jax import lax
from jax.experimental import pallas as pl
from jax.experimental.pallas import tpu as pltpu
from jax.sharding import PartitionSpec as P

MESH = pl.DeviceIdType.MESH
F32 = jnp.float32
BF16 = jnp.bfloat16

SHIFTS = (0, 1, -2, 3, -4, 5, -6, 7, 8)
PLANE = ((0, 0), (0, 1), (0, 3), (1, 0), (3, 0), (1, 1), (1, 3), (3, 1),
         (3, 3), (0, 2), (2, 0), (1, 2), (3, 2), (2, 1), (2, 3), (2, 2))
NB = 16
NC = 9
BLK = 256
PROJ = 32
ROWS = NB * BLK
COLS = NC * BLK
DEEP = 256
CHUNK = 1024
GROUP = 768
LANES = 128
SCALE = math.sqrt(4.0 / PROJ * math.log2(math.e))
NOISE = 0.5
DIAG = 1.0 + NOISE


NEAREST_LAST = sorted(
    ((dy, dx, dc) for dy in range(4) for dx in range(4) for dc in range(2)),
    key=lambda d: (-min(d[0], 4 - d[0]) - min(d[1], 4 - d[1]), -d[2]))


def place():
    w = lax.axis_index("wide")
    n = lax.axis_index("narrow")
    z = w // 8
    y = (w // 2) % 4
    x = (w % 2) * 2 + n // 2
    core = n % 2
    return z * 2 + core, y, x


def device(a, y, x):
    z = a // 2
    core = a % 2
    return ((z * 4 + y) * 2 + x // 2, (x % 2) * 2 + core)


def body(feat_hbm, proj_hbm, targ_ref, out_ref,
         feat, proj, lat_row, lat_col, t_row, t_col, o_row, o_col,
         side_a, side_b, wide_u, tiles, row_acc, col_acc,
         rp1, cp1, rr1, cr1, rp2, cp2, rr2, cr2,
         sc_out, sc_in, load_sem, lat_send, lat_rrecv, lat_crecv,
         small_send, small_recv, t_rrecv, t_crecv, o_rrecv, o_crecv):
    a, y, x = place()

    def along_row(j, sign):
        dy, dx = PLANE[j]
        return device(a, (y + sign * dy + 4) % 4, (x + sign * dx + 4) % 4)

    def along_col(shift):
        return device((a + shift + 32) % 16, y, x)

    def send(src, dst, ssem, rsem, where):
        pltpu.make_async_remote_copy(
            src_ref=src, dst_ref=dst, send_sem=ssem, recv_sem=rsem,
            device_id=where, device_id_type=MESH).start()

    def settle(ref, sem):
        pltpu.make_async_copy(ref, ref, sem).wait()

    halves = [pl.ds(0, 1024), pl.ds(1024, 1024)]
    load_p = pltpu.make_async_copy(proj_hbm, proj, load_sem.at[0])
    load_f = [pltpu.make_async_copy(feat_hbm.at[:, h], feat.at[:, h], load_sem.at[1 + i])
              for i, h in enumerate(halves)]
    load_p.start()
    for load in load_f:
        load.start()

    barrier = pltpu.get_barrier_semaphore()
    for j in range(NB - 1, 0, -1):
        pl.semaphore_signal(barrier, inc=1, device_id=along_row(j, 1), device_id_type=MESH)
        if j < NC:
            pl.semaphore_signal(barrier, inc=1, device_id=along_col(SHIFTS[j]),
                                device_id_type=MESH)
    t_row[0] = targ_ref[...]
    t_col[0] = targ_ref[...]
    def spread(values, j):
        for h in range(BLK // LANES):
            piece = values[:, h * LANES:(h + 1) * LANES]
            wide_u[j * BLK + h * LANES:j * BLK + (h + 1) * LANES, :] = jnp.transpose(
                jnp.broadcast_to(piece, (LANES, LANES)))

    def split(v):
        h = v.astype(BF16)
        rest = v - h.astype(F32)
        m = rest.astype(BF16)
        l = (rest - m.astype(F32)).astype(BF16)
        return h, m, l

    line = lax.broadcasted_iota(jnp.int32, (16, BLK), 0)

    def parts(v):
        h, m, l = split(v)
        half = jnp.sum(v * v, axis=0, keepdims=True) * -0.5
        qh, qm, ql = (jnp.broadcast_to(q.astype(F32), (16, BLK)) for q in split(half))
        return h, m, l, qh, qm, ql

    def extra(qh, qm, ql, first):
        one = jnp.where((line >= 3 - first) & (line < 6 - first), 1.0, 0.0)
        e = jnp.where(line == first, qh, jnp.where(line == first + 1, qm,
                                                   jnp.where(line == first + 2, ql, one)))
        return e.astype(BF16)

    zeros = jnp.zeros((DEEP - 6 * PROJ - 16, BLK), BF16)

    def build_a(j):
        h, m, l, qh, qm, ql = parts(lat_row[j])
        stack = jnp.concatenate([h, h, m, m, h, l, extra(qh, qm, ql, 0), zeros], axis=0)
        side_a[j * BLK:(j + 1) * BLK, :] = jnp.transpose(stack)

    def build_b(k):
        h, m, l, qh, qm, ql = parts(lat_row[0] if k == 0 else lat_col[k])
        side_b[:, k * BLK:(k + 1) * BLK] = jnp.concatenate(
            [h, m, h, m, l, h, extra(qh, qm, ql, 3), zeros], axis=0)

    load_p.wait()
    latent = jnp.zeros((PROJ, BLK), F32)
    for load, h in zip(load_f, halves):
        load.wait()
        latent = latent + lax.dot_general(proj[:, h], feat[:, h], (((1,), (1,)), ((), ())),
                                          preferred_element_type=F32)
    lat_row[0] = latent * SCALE
    pl.semaphore_wait(barrier, NB + NC - 2)

    for j in range(1, NB):
        send(targ_ref, t_row.at[j], small_send.at[0], t_rrecv.at[j // 4], along_row(j, -1))
        if j < NC:
            send(targ_ref, t_col.at[j], small_send.at[1], t_crecv.at[j // 3],
                 along_col(-SHIFTS[j]))
    for j in range(1, NC):
        send(lat_row.at[0], lat_col.at[j], lat_send.at[1], lat_crecv.at[j],
             along_col(-SHIFTS[j]))
    for j in range(1, NB):
        send(lat_row.at[0], lat_row.at[j], lat_send.at[0], lat_rrecv.at[j], along_row(j, -1))

    build_a(0)
    build_b(0)
    spread(t_row[0], 0)

    def fold_rows(r, out):
        for i in range(CHUNK // LANES):
            lo = r * CHUNK + i * LANES
            sums = jnp.sum(jnp.transpose(row_acc[lo:lo + LANES, :]), axis=0, keepdims=True)
            out[lo // BLK, :, (lo % BLK):(lo % BLK) + LANES] = sums

    def send_rows(r, out, into, sem):
        for j in range(4 * r, 4 * r + 4):
            if j:
                send(out.at[j], into.at[j], small_send.at[sem], small_recv.at[sem],
                     along_row(j, 1))

    def send_cols(ks, out, into, sem):
        for k in ks:
            if k:
                send(out.at[k], into.at[k], small_send.at[sem], small_recv.at[sem],
                     along_col(SHIFTS[k]))

    told, ready_r, ready_c = set(), {0}, {0}
    begun_r, begun_c = set(), set()

    def slots(i, width):
        return range(max(width * i, 1), width * i + width)

    def span(ref, i, width):
        near = slots(i, width)
        return ref.at[pl.ds(near[0], len(near))]

    def step(low, high, left, right):
        for j in range(low, high):
            if ("r", j // 4) not in told:
                told.add(("r", j // 4))
                settle(span(t_row, j // 4, 4), t_rrecv.at[j // 4])
        for k in range(left, right):
            if ("c", k // 3) not in told:
                told.add(("c", k // 3))
                settle(span(t_col, k // 3, 3), t_crecv.at[k // 3])
        for j in range(low, high):
            if j not in ready_r:
                spread(t_row[j], j)
        for k in range(left, right):
            if k not in ready_c:
                ready_c.add(k)
                settle(lat_col.at[k], lat_crecv.at[k])
                build_b(k)
        for j in range(low, high):
            if j not in ready_r:
                ready_r.add(j)
                settle(lat_row.at[j], lat_rrecv.at[j])
                build_a(j)
        rows = slice(low * BLK, high * BLK)
        cols = slice(left * BLK, right * BLK)
        power = jnp.dot(side_a[rows, :], side_b[:, cols], preferred_element_type=F32)
        p = jnp.exp2(power)
        tiles[rows, cols] = p
        u = wide_u[rows, :]
        total = None
        for i in range((right - left) * BLK // LANES):
            lane = left * BLK + i * LANES
            k = lane // BLK
            piece = p[:, i * LANES:(i + 1) * LANES]
            down = jnp.sum((piece * u).reshape((high - low) * BLK // 8, 8, LANES), axis=0)
            if k not in begun_c:
                col_acc[:, lane:lane + LANES] = down
            else:
                col_acc[:, lane:lane + LANES] += down
            if k not in (0, NC - 1):
                v = t_col[k, :, (lane % BLK):(lane % BLK) + LANES]
                total = piece * v if total is None else total + piece * v
        begun_c.update(range(left, right))
        if total is not None:
            if low in begun_r:
                row_acc[rows, :] += total
            else:
                row_acc[rows, :] = total
            begun_r.update(range(low, high))

    def fold_cols(ks, out):
        for k in ks:
            out[k] = jnp.sum(col_acc[:, k * BLK:(k + 1) * BLK], axis=0, keepdims=True)

    order = ((0, 4, 0, 3), (4, 8, 0, 3), (8, 12, 0, 3), (12, 14, 0, 3), (0, 4, 3, 6), (4, 8, 3, 6), (8, 14, 3, 6),
             (0, 8, 6, 9), (8, 14, 6, 9), (14, 16, 0, 9))
    sent_r = set()
    for i, (low, high, left, right) in enumerate(order):
        step(low, high, left, right)
        later = order[i + 1:]
        for k in range(left, right):
            if all(not l <= k < h for _, _, l, h in later):
                fold_cols([k], cp1)
                send_cols([k], cp1, cr1, 3)
        rest = [(b, e) for b, e, l, _ in later if l < NC - 1]
        for r in range(4):
            if r not in sent_r and all(e <= 4 * r or 4 * r + 4 <= b for b, e in rest):
                sent_r.add(r)
                fold_rows(r, rp1)
                send_rows(r, rp1, rr1, 2)

    def gathered(rp, rr, cp, cr, own):
        settle(rr.at[pl.ds(1, NB - 1)], small_recv.at[2 if own else 4])
        settle(cr.at[pl.ds(1, NC - 1)], small_recv.at[3 if own else 5])
        total = rp[0] + cp[0]
        for j in range(1, NB):
            total = total + rr[j]
        for k in range(1, NC):
            total = total + cr[k]
        return total

    t = targ_ref[...]
    off = gathered(rp1, rr1, cp1, cr1, True) - t
    o_row[0] = off
    o_col[0] = off
    for j in range(1, NB):
        send(o_row.at[0], o_row.at[j], small_send.at[6], o_rrecv.at[j // 4], along_row(j, -1))
        if j < NC:
            send(o_col.at[0], o_col.at[j], small_send.at[7], o_crecv.at[j // 5],
                 along_col(-SHIFTS[j]))

    lane = lax.broadcasted_iota(jnp.int32, (1, LANES), 1)
    z, core = a // 2, a % 2
    ys = [(y + d) % 4 for d in range(4)]
    xs = [(x + d) % 4 for d in range(4)]
    cores = [core, 1 - core]

    def across(v):
        return jnp.sum(v, axis=1, keepdims=True)

    def share(slot, values, between=None):
        line = jnp.zeros((1, LANES), F32)
        for i, v in enumerate(values):
            line = jnp.where(lane == i, v, line)
        sc_out[slot] = line

        def plane(q, last):
            far = 4 + (1 - 2 * (q % 2)) * ((q + 1) // 2)
            base = ((z + far) % 8) * 4
            for i, (dy, dx, dc) in enumerate(NEAREST_LAST):
                if last and (dy, dx, dc) == (0, 0, 0):
                    continue
                where = ((base + ys[dy]) * 2 + xs[dx] // 2, (xs[dx] % 2) * 2 + cores[dc])
                send(sc_out.at[slot], sc_in.at[slot, q * 32 + i], small_send.at[8 + slot],
                     small_recv.at[8 + slot], where)

        def one(q, carry):
            plane(q, False)
            return carry

        lax.fori_loop(0, 4, one, 0)
        if between is not None:
            between()
        lax.fori_loop(4, 7, one, 0)
        plane(7, True)

    def shared(slot):
        settle(sc_in.at[slot, pl.ds(0, 255)], small_recv.at[8 + slot])
        sums = [sc_out[slot]] + [sc_in[slot, i] for i in range(255)]
        while len(sums) > 1:
            sums = [p + q for p, q in zip(sums[::2], sums[1::2])] + sums[len(sums) & ~1:]
        return [sums[0][:, i:i + 1] for i in range(3)]

    share(0, (across(t * t), across(t * off), across(off * off)))

    TAKE = 64
    every = range(COLS // LANES)
    near, far = every[:10], every[10:]
    lane_v, downs = {}, {}

    def look(lanes):
        for l in lanes:
            downs[l] = jnp.zeros((8, LANES), F32)
            if 2 <= l < 16:
                lane_v[l] = jnp.broadcast_to(
                    o_col[l // 2, :, (l % 2) * LANES:(l % 2) * LANES + LANES], (8, LANES))

    def sweep(r, lanes, first):
        def some(i, carry):
            start = pl.multiple_of(r * CHUNK + i * TAKE, TAKE)
            carry = list(carry)
            for g in range(TAKE // 8):
                at = pl.ds(start + g * 8, 8)
                u = wide_u[at, :]
                total = None if first else row_acc[at, :]
                for n, l in enumerate(lanes):
                    piece = tiles[at, l * LANES:(l + 1) * LANES]
                    carry[n] = carry[n] + piece * u
                    if l in lane_v:
                        w = piece * lane_v[l]
                        total = w if total is None else total + w
                row_acc[at, :] = total
            return tuple(carry)

        done = lax.fori_loop(0, CHUNK // TAKE, some, tuple(downs[l] for l in lanes))
        downs.update(zip(lanes, done))

    def arrive(r):
        settle(span(o_row, r, 4), o_rrecv.at[r])
        for j in range(4 * r, 4 * r + 4):
            spread(o_row[j], j)

    quad = jnp.zeros((1, BLK), F32)

    def leave(r, quad):
        fold_rows(r, rp2)
        if r < 3:
            send_rows(r, rp2, rr2, 4)
        for j in range(4 * r, 4 * r + 4):
            quad = quad + o_row[j] * rp2[j]
        return quad

    settle(o_col.at[pl.ds(1, 4)], o_crecv.at[0])
    look(near)
    arrive(0)
    sweep(0, near, True)
    arrive(1)
    sweep(1, near, True)
    settle(o_col.at[pl.ds(5, 4)], o_crecv.at[1])
    look(far)
    sweep(0, far, False)
    quad = leave(0, quad)
    sweep(1, far, False)
    quad = leave(1, quad)
    arrive(2)
    sweep(2, every, True)
    quad = leave(2, quad)
    arrive(3)

    s0, s1, s2 = shared(0)
    below = DIAG * s0 + s1
    alpha = s0 / below
    gamma = s1 / below
    resid = gamma * t - alpha * off
    norm_own, cross_own = across(resid * resid), across(resid * t)

    sweep(3, every, True)
    for k in range(NC):
        cp2[k] = jnp.concatenate([jnp.sum(downs[2 * k], axis=0, keepdims=True),
                                  jnp.sum(downs[2 * k + 1], axis=0, keepdims=True)], axis=1)
    quad = leave(3, quad)
    for k in range(NC):
        quad = quad + o_col[k] * cp2[k]

    def last_parts():
        send_rows(3, rp2, rr2, 4)
        send_cols(range(NC), cp2, cr2, 5)

    share(1, (norm_own, cross_own, across(quad)), last_parts)
    product = gathered(rp2, rr2, cp2, cr2, False) - off
    settle(t_row.at[pl.ds(1, NB - 1)], small_send.at[0])
    settle(t_col.at[pl.ds(1, NC - 1)], small_send.at[1])
    settle(lat_row.at[pl.ds(1, NB - 1)], lat_send.at[0])
    settle(lat_col.at[pl.ds(1, NC - 1)], lat_send.at[1])
    settle(rr1.at[pl.ds(1, NB - 1)], small_send.at[2])
    settle(cr1.at[pl.ds(1, NC - 1)], small_send.at[3])
    settle(rr2.at[pl.ds(1, NB - 1)], small_send.at[4])
    settle(cr2.at[pl.ds(1, NC - 1)], small_send.at[5])
    settle(o_row.at[pl.ds(1, NB - 1)], small_send.at[6])
    settle(o_col.at[pl.ds(1, NC - 1)], small_send.at[7])
    for slot in range(2):
        settle(sc_in.at[slot, pl.ds(0, 255)], small_send.at[8 + slot])

    n1, cross, s3 = shared(1)
    beta = n1 / s0
    both = gamma + beta
    length = n1 + 2.0 * beta * cross + beta * beta * s0
    energy = (DIAG * length + both * both * s1 - 2.0 * alpha * both * s2
              + alpha * alpha * (s3 - s2))
    step2 = n1 / energy
    direction = resid + beta * t
    image = DIAG * direction + both * off - alpha * product
    out_ref[0] = alpha * t
    out_ref[1] = step2 * direction
    out_ref[2] = resid
    out_ref[3] = step2 * image


def on_device(features, projection, targets):
    vm = pl.BlockSpec(memory_space=pltpu.VMEM)
    hbm = pl.BlockSpec(memory_space=pl.ANY)
    dma = pltpu.SemaphoreType.DMA
    terms = pl.pallas_call(
        body,
        out_shape=jax.ShapeDtypeStruct((4, 1, BLK), F32),
        in_specs=[hbm, hbm, vm],
        out_specs=vm,
        scratch_shapes=[
            pltpu.VMEM((BLK, 2048), BF16), pltpu.VMEM((PROJ, 2048), BF16),
            pltpu.VMEM((NB, PROJ, BLK), F32), pltpu.VMEM((NC, PROJ, BLK), F32),
            pltpu.VMEM((NB, 1, BLK), F32), pltpu.VMEM((NC, 1, BLK), F32),
            pltpu.VMEM((NB, 1, BLK), F32), pltpu.VMEM((NC, 1, BLK), F32),
            pltpu.VMEM((ROWS, DEEP), BF16), pltpu.VMEM((DEEP, COLS), BF16),
            pltpu.VMEM((ROWS, LANES), F32), pltpu.VMEM((ROWS, COLS), F32),
            pltpu.VMEM((ROWS, LANES), F32), pltpu.VMEM((8, COLS), F32),
            pltpu.VMEM((NB, 1, BLK), F32), pltpu.VMEM((NC, 1, BLK), F32),
            pltpu.VMEM((NB, 1, BLK), F32), pltpu.VMEM((NC, 1, BLK), F32),
            pltpu.VMEM((NB, 1, BLK), F32), pltpu.VMEM((NC, 1, BLK), F32),
            pltpu.VMEM((NB, 1, BLK), F32), pltpu.VMEM((NC, 1, BLK), F32),
            pltpu.VMEM((2, 1, LANES), F32), pltpu.VMEM((2, 256, 1, LANES), F32),
            dma((3,)), dma((2,)), dma((NB,)), dma((NC,)),
            dma((10,)), dma((10,)), dma((4,)), dma((3,)), dma((4,)), dma((2,)),
        ],
        compiler_params=pltpu.CompilerParams(
            collective_id=0, has_side_effects=True, vmem_limit_bytes=60 * 2**20),
        name="conjugate",
    )(features, projection.T, targets.reshape(1, BLK))
    terms = terms.reshape(4, BLK)
    return terms[0] + terms[1], terms[2] - terms[3]


def solution(mesh):
    in_specs = (P(("wide", "narrow"), None), P(), P(("wide", "narrow")))
    out_specs = (P(("wide", "narrow")), P(("wide", "narrow")))
    return jax.shard_map(
        on_device, mesh=mesh, in_specs=in_specs, out_specs=out_specs, check_vma=False)
```

```python
import functools
import math

import jax
import jax.numpy as jnp
from jax import lax
from jax.experimental import pallas as pl
from jax.experimental.pallas import tpu as pltpu
from jax.sharding import PartitionSpec as P

MESH = pl.DeviceIdType.MESH
F32 = jnp.float32
BF16 = jnp.bfloat16

SHIFTS = (0, 1, -2, 3, -4, 5, -6, 7, 8)
PLANE = ((0, 0), (0, 1), (0, 3), (1, 0), (3, 0), (1, 1), (1, 3), (3, 1),
         (3, 3), (0, 2), (2, 0), (1, 2), (3, 2), (2, 1), (2, 3), (2, 2))
NB = 16
NC = 9
BLK = 256
PROJ = 32
ROWS = NB * BLK
COLS = NC * BLK
DEEP = 256
CHUNK = 1024
GROUP = 768
LANES = 128
SCALE = math.sqrt(4.0 / PROJ * math.log2(math.e))
NOISE = 0.5
DIAG = 1.0 + NOISE


NEAREST_LAST = sorted(
    ((dy, dx, dc) for dy in range(4) for dx in range(4) for dc in range(2)),
    key=lambda d: (-min(d[0], 4 - d[0]) - min(d[1], 4 - d[1]), -d[2]))


def place():
    w = lax.axis_index("wide")
    n = lax.axis_index("narrow")
    z = w // 8
    y = (w // 2) % 4
    x = (w % 2) * 2 + n // 2
    core = n % 2
    return z * 2 + core, y, x


def device(a, y, x):
    z = a // 2
    core = a % 2
    return ((z * 4 + y) * 2 + x // 2, (x % 2) * 2 + core)


def body(feat_hbm, proj_hbm, targ_ref, out_ref,
         feat, proj, lat_row, lat_col, t_row, t_col, o_row, o_col,
         side_a, side_b, wide_u, tiles, row_acc, col_acc,
         rp1, cp1, rr1, cr1, rp2, cp2, rr2, cr2,
         sc_out, sc_in, load_sem, lat_send, lat_rrecv, lat_crecv,
         small_send, small_recv, t_rrecv, t_crecv, o_rrecv, o_crecv):
    a, y, x = place()

    def along_row(j, sign):
        dy, dx = PLANE[j]
        return device(a, (y + sign * dy + 4) % 4, (x + sign * dx + 4) % 4)

    def along_col(shift):
        return device((a + shift + 32) % 16, y, x)

    def send(src, dst, ssem, rsem, where):
        pltpu.make_async_remote_copy(
            src_ref=src, dst_ref=dst, send_sem=ssem, recv_sem=rsem,
            device_id=where, device_id_type=MESH).start()

    def settle(ref, sem):
        pltpu.make_async_copy(ref, ref, sem).wait()

    halves = [pl.ds(0, 1024), pl.ds(1024, 1024)]
    load_p = pltpu.make_async_copy(proj_hbm, proj, load_sem.at[0])
    load_f = [pltpu.make_async_copy(feat_hbm.at[:, h], feat.at[:, h], load_sem.at[1 + i])
              for i, h in enumerate(halves)]
    load_p.start()
    for load in load_f:
        load.start()

    barrier = pltpu.get_barrier_semaphore()
    for j in range(NB - 1, 0, -1):
        pl.semaphore_signal(barrier, inc=1, device_id=along_row(j, 1), device_id_type=MESH)
        if j < NC:
            pl.semaphore_signal(barrier, inc=1, device_id=along_col(SHIFTS[j]),
                                device_id_type=MESH)
    t_row[0] = targ_ref[...]
    t_col[0] = targ_ref[...]
    def spread(values, j):
        for h in range(BLK // LANES):
            piece = values[:, h * LANES:(h + 1) * LANES]
            wide_u[j * BLK + h * LANES:j * BLK + (h + 1) * LANES, :] = jnp.transpose(
                jnp.broadcast_to(piece, (LANES, LANES)))

    def split(v):
        h = v.astype(BF16)
        rest = v - h.astype(F32)
        m = rest.astype(BF16)
        l = (rest - m.astype(F32)).astype(BF16)
        return h, m, l

    line = lax.broadcasted_iota(jnp.int32, (16, BLK), 0)

    def parts(v):
        h, m, l = split(v)
        half = jnp.sum(v * v, axis=0, keepdims=True) * -0.5
        qh, qm, ql = (jnp.broadcast_to(q.astype(F32), (16, BLK)) for q in split(half))
        return h, m, l, qh, qm, ql

    def extra(qh, qm, ql, first):
        one = jnp.where((line >= 3 - first) & (line < 6 - first), 1.0, 0.0)
        e = jnp.where(line == first, qh, jnp.where(line == first + 1, qm,
                                                   jnp.where(line == first + 2, ql, one)))
        return e.astype(BF16)

    zeros = jnp.zeros((DEEP - 6 * PROJ - 16, BLK), BF16)

    def build_a(j):
        h, m, l, qh, qm, ql = parts(lat_row[j])
        stack = jnp.concatenate([h, h, m, m, h, l, extra(qh, qm, ql, 0), zeros], axis=0)
        side_a[j * BLK:(j + 1) * BLK, :] = jnp.transpose(stack)

    def build_b(k):
        h, m, l, qh, qm, ql = parts(lat_row[0] if k == 0 else lat_col[k])
        side_b[:, k * BLK:(k + 1) * BLK] = jnp.concatenate(
            [h, m, h, m, l, h, extra(qh, qm, ql, 3), zeros], axis=0)

    load_p.wait()
    latent = jnp.zeros((PROJ, BLK), F32)
    for load, h in zip(load_f, halves):
        load.wait()
        latent = latent + lax.dot_general(proj[:, h], feat[:, h], (((1,), (1,)), ((), ())),
                                          preferred_element_type=F32)
    lat_row[0] = latent * SCALE
    pl.semaphore_wait(barrier, NB + NC - 2)

    for j in range(1, NB):
        send(targ_ref, t_row.at[j], small_send.at[0], t_rrecv.at[j // 4], along_row(j, -1))
        if j < NC:
            send(targ_ref, t_col.at[j], small_send.at[1], t_crecv.at[j // 3],
                 along_col(-SHIFTS[j]))
    for j in range(1, NC):
        send(lat_row.at[0], lat_col.at[j], lat_send.at[1], lat_crecv.at[j],
             along_col(-SHIFTS[j]))
    for j in range(1, NB):
        send(lat_row.at[0], lat_row.at[j], lat_send.at[0], lat_rrecv.at[j], along_row(j, -1))

    build_a(0)
    build_b(0)
    spread(t_row[0], 0)

    def fold_rows(r, out):
        for i in range(CHUNK // LANES):
            lo = r * CHUNK + i * LANES
            sums = jnp.sum(jnp.transpose(row_acc[lo:lo + LANES, :]), axis=0, keepdims=True)
            out[lo // BLK, :, (lo % BLK):(lo % BLK) + LANES] = sums

    def send_rows(r, out, into, sem):
        for j in range(4 * r, 4 * r + 4):
            if j:
                send(out.at[j], into.at[j], small_send.at[sem], small_recv.at[sem],
                     along_row(j, 1))

    def send_cols(ks, out, into, sem):
        for k in ks:
            if k:
                send(out.at[k], into.at[k], small_send.at[sem], small_recv.at[sem],
                     along_col(SHIFTS[k]))

    told, ready_r, ready_c = set(), {0}, {0}
    begun_r, begun_c = set(), set()

    def slots(i, width):
        return range(max(width * i, 1), width * i + width)

    def span(ref, i, width):
        near = slots(i, width)
        return ref.at[pl.ds(near[0], len(near))]

    def step(low, high, left, right):
        for j in range(low, high):
            if ("r", j // 4) not in told:
                told.add(("r", j // 4))
                settle(span(t_row, j // 4, 4), t_rrecv.at[j // 4])
        for k in range(left, right):
            if ("c", k // 3) not in told:
                told.add(("c", k // 3))
                settle(span(t_col, k // 3, 3), t_crecv.at[k // 3])
        for j in range(low, high):
            if j not in ready_r:
                spread(t_row[j], j)
        for k in range(left, right):
            if k not in ready_c:
                ready_c.add(k)
                settle(lat_col.at[k], lat_crecv.at[k])
                build_b(k)
        for j in range(low, high):
            if j not in ready_r:
                ready_r.add(j)
                settle(lat_row.at[j], lat_rrecv.at[j])
                build_a(j)
        rows = slice(low * BLK, high * BLK)
        cols = slice(left * BLK, right * BLK)
        power = jnp.dot(side_a[rows, :], side_b[:, cols], preferred_element_type=F32)
        p = jnp.exp2(power)
        tiles[rows, cols] = p
        u = wide_u[rows, :]
        total = None
        for i in range((right - left) * BLK // LANES):
            lane = left * BLK + i * LANES
            k = lane // BLK
            piece = p[:, i * LANES:(i + 1) * LANES]
            down = jnp.sum((piece * u).reshape((high - low) * BLK // 8, 8, LANES), axis=0)
            if k not in begun_c:
                col_acc[:, lane:lane + LANES] = down
            else:
                col_acc[:, lane:lane + LANES] += down
            if k not in (0, NC - 1):
                v = t_col[k, :, (lane % BLK):(lane % BLK) + LANES]
                total = piece * v if total is None else total + piece * v
        begun_c.update(range(left, right))
        if total is not None:
            if low in begun_r:
                row_acc[rows, :] += total
            else:
                row_acc[rows, :] = total
            begun_r.update(range(low, high))

    def fold_cols(ks, out):
        for k in ks:
            out[k] = jnp.sum(col_acc[:, k * BLK:(k + 1) * BLK], axis=0, keepdims=True)

    order = ((0, 4, 0, 3), (4, 8, 0, 3), (8, 12, 0, 3), (0, 4, 3, 6), (4, 8, 3, 6), (8, 12, 3, 6),
             (12, 14, 0, 6), (0, 8, 6, 8), (8, 14, 6, 8), (14, 16, 0, 8), (0, 8, 8, 9), (8, 16, 8, 9))
    sent_r = set()
    for i, (low, high, left, right) in enumerate(order):
        step(low, high, left, right)
        later = order[i + 1:]
        for k in range(left, right):
            if all(not l <= k < h for _, _, l, h in later):
                fold_cols([k], cp1)
                send_cols([k], cp1, cr1, 3)
        rest = [(b, e) for b, e, l, _ in later if l < NC - 1]
        for r in range(4):
            if r not in sent_r and all(e <= 4 * r or 4 * r + 4 <= b for b, e in rest):
                sent_r.add(r)
                fold_rows(r, rp1)
                send_rows(r, rp1, rr1, 2)

    def gathered(rp, rr, cp, cr, own):
        settle(rr.at[pl.ds(1, NB - 1)], small_recv.at[2 if own else 4])
        settle(cr.at[pl.ds(1, NC - 1)], small_recv.at[3 if own else 5])
        total = rp[0] + cp[0]
        for j in range(1, NB):
            total = total + rr[j]
        for k in range(1, NC):
            total = total + cr[k]
        return total

    t = targ_ref[...]
    off = gathered(rp1, rr1, cp1, cr1, True) - t
    o_row[0] = off
    o_col[0] = off
    for j in range(1, NB):
        send(o_row.at[0], o_row.at[j], small_send.at[6], o_rrecv.at[j // 4], along_row(j, -1))
        if j < NC:
            send(o_col.at[0], o_col.at[j], small_send.at[7], o_crecv.at[j // 5],
                 along_col(-SHIFTS[j]))

    lane = lax.broadcasted_iota(jnp.int32, (1, LANES), 1)
    z, core = a // 2, a % 2
    ys = [(y + d) % 4 for d in range(4)]
    xs = [(x + d) % 4 for d in range(4)]
    cores = [core, 1 - core]

    def across(v):
        return jnp.sum(v, axis=1, keepdims=True)

    def share(slot, values, between=None):
        line = jnp.zeros((1, LANES), F32)
        for i, v in enumerate(values):
            line = jnp.where(lane == i, v, line)
        sc_out[slot] = line

        def plane(q, last):
            far = 4 + (1 - 2 * (q % 2)) * ((q + 1) // 2)
            base = ((z + far) % 8) * 4
            for i, (dy, dx, dc) in enumerate(NEAREST_LAST):
                if last and (dy, dx, dc) == (0, 0, 0):
                    continue
                where = ((base + ys[dy]) * 2 + xs[dx] // 2, (xs[dx] % 2) * 2 + cores[dc])
                send(sc_out.at[slot], sc_in.at[slot, q * 32 + i], small_send.at[8 + slot],
                     small_recv.at[8 + slot], where)

        def one(q, carry):
            plane(q, False)
            return carry

        lax.fori_loop(0, 4, one, 0)
        if between is not None:
            between()
        lax.fori_loop(4, 7, one, 0)
        plane(7, True)

    def shared(slot):
        settle(sc_in.at[slot, pl.ds(0, 255)], small_recv.at[8 + slot])
        sums = [sc_out[slot]] + [sc_in[slot, i] for i in range(255)]
        while len(sums) > 1:
            sums = [p + q for p, q in zip(sums[::2], sums[1::2])] + sums[len(sums) & ~1:]
        return [sums[0][:, i:i + 1] for i in range(3)]

    share(0, (across(t * t), across(t * off), across(off * off)))

    TAKE = 64
    every = range(COLS // LANES)
    near, far = every[:10], every[10:]
    lane_v, downs = {}, {}

    def look(lanes):
        for l in lanes:
            downs[l] = jnp.zeros((8, LANES), F32)
            if 2 <= l < 16:
                lane_v[l] = jnp.broadcast_to(
                    o_col[l // 2, :, (l % 2) * LANES:(l % 2) * LANES + LANES], (8, LANES))

    def sweep(r, lanes, first):
        def some(i, carry):
            start = pl.multiple_of(r * CHUNK + i * TAKE, TAKE)
            carry = list(carry)
            for g in range(TAKE // 8):
                at = pl.ds(start + g * 8, 8)
                u = wide_u[at, :]
                total = None if first else row_acc[at, :]
                for n, l in enumerate(lanes):
                    piece = tiles[at, l * LANES:(l + 1) * LANES]
                    carry[n] = carry[n] + piece * u
                    if l in lane_v:
                        w = piece * lane_v[l]
                        total = w if total is None else total + w
                row_acc[at, :] = total
            return tuple(carry)

        done = lax.fori_loop(0, CHUNK // TAKE, some, tuple(downs[l] for l in lanes))
        downs.update(zip(lanes, done))

    def arrive(r):
        settle(span(o_row, r, 4), o_rrecv.at[r])
        for j in range(4 * r, 4 * r + 4):
            spread(o_row[j], j)

    quad = jnp.zeros((1, BLK), F32)

    def leave(r, quad):
        fold_rows(r, rp2)
        if r < 3:
            send_rows(r, rp2, rr2, 4)
        for j in range(4 * r, 4 * r + 4):
            quad = quad + o_row[j] * rp2[j]
        return quad

    settle(o_col.at[pl.ds(1, 4)], o_crecv.at[0])
    look(near)
    arrive(0)
    sweep(0, near, True)
    arrive(1)
    sweep(1, near, True)
    settle(o_col.at[pl.ds(5, 4)], o_crecv.at[1])
    look(far)
    sweep(0, far, False)
    quad = leave(0, quad)
    sweep(1, far, False)
    quad = leave(1, quad)
    arrive(2)
    sweep(2, every, True)
    quad = leave(2, quad)
    arrive(3)

    s0, s1, s2 = shared(0)
    below = DIAG * s0 + s1
    alpha = s0 / below
    gamma = s1 / below
    resid = gamma * t - alpha * off
    norm_own, cross_own = across(resid * resid), across(resid * t)

    sweep(3, every, True)
    for k in range(NC):
        cp2[k] = jnp.concatenate([jnp.sum(downs[2 * k], axis=0, keepdims=True),
                                  jnp.sum(downs[2 * k + 1], axis=0, keepdims=True)], axis=1)
    quad = leave(3, quad)
    for k in range(NC):
        quad = quad + o_col[k] * cp2[k]

    def last_parts():
        send_rows(3, rp2, rr2, 4)
        send_cols(range(NC), cp2, cr2, 5)

    share(1, (norm_own, cross_own, across(quad)), last_parts)
    product = gathered(rp2, rr2, cp2, cr2, False) - off
    settle(t_row.at[pl.ds(1, NB - 1)], small_send.at[0])
    settle(t_col.at[pl.ds(1, NC - 1)], small_send.at[1])
    settle(lat_row.at[pl.ds(1, NB - 1)], lat_send.at[0])
    settle(lat_col.at[pl.ds(1, NC - 1)], lat_send.at[1])
    settle(rr1.at[pl.ds(1, NB - 1)], small_send.at[2])
    settle(cr1.at[pl.ds(1, NC - 1)], small_send.at[3])
    settle(rr2.at[pl.ds(1, NB - 1)], small_send.at[4])
    settle(cr2.at[pl.ds(1, NC - 1)], small_send.at[5])
    settle(o_row.at[pl.ds(1, NB - 1)], small_send.at[6])
    settle(o_col.at[pl.ds(1, NC - 1)], small_send.at[7])
    for slot in range(2):
        settle(sc_in.at[slot, pl.ds(0, 255)], small_send.at[8 + slot])

    n1, cross, s3 = shared(1)
    beta = n1 / s0
    both = gamma + beta
    length = n1 + 2.0 * beta * cross + beta * beta * s0
    energy = (DIAG * length + both * both * s1 - 2.0 * alpha * both * s2
              + alpha * alpha * (s3 - s2))
    step2 = n1 / energy
    direction = resid + beta * t
    image = DIAG * direction + both * off - alpha * product
    out_ref[0] = alpha * t
    out_ref[1] = step2 * direction
    out_ref[2] = resid
    out_ref[3] = step2 * image


def on_device(features, projection, targets):
    vm = pl.BlockSpec(memory_space=pltpu.VMEM)
    hbm = pl.BlockSpec(memory_space=pl.ANY)
    dma = pltpu.SemaphoreType.DMA
    terms = pl.pallas_call(
        body,
        out_shape=jax.ShapeDtypeStruct((4, 1, BLK), F32),
        in_specs=[hbm, hbm, vm],
        out_specs=vm,
        scratch_shapes=[
            pltpu.VMEM((BLK, 2048), BF16), pltpu.VMEM((PROJ, 2048), BF16),
            pltpu.VMEM((NB, PROJ, BLK), F32), pltpu.VMEM((NC, PROJ, BLK), F32),
            pltpu.VMEM((NB, 1, BLK), F32), pltpu.VMEM((NC, 1, BLK), F32),
            pltpu.VMEM((NB, 1, BLK), F32), pltpu.VMEM((NC, 1, BLK), F32),
            pltpu.VMEM((ROWS, DEEP), BF16), pltpu.VMEM((DEEP, COLS), BF16),
            pltpu.VMEM((ROWS, LANES), F32), pltpu.VMEM((ROWS, COLS), F32),
            pltpu.VMEM((ROWS, LANES), F32), pltpu.VMEM((8, COLS), F32),
            pltpu.VMEM((NB, 1, BLK), F32), pltpu.VMEM((NC, 1, BLK), F32),
            pltpu.VMEM((NB, 1, BLK), F32), pltpu.VMEM((NC, 1, BLK), F32),
            pltpu.VMEM((NB, 1, BLK), F32), pltpu.VMEM((NC, 1, BLK), F32),
            pltpu.VMEM((NB, 1, BLK), F32), pltpu.VMEM((NC, 1, BLK), F32),
            pltpu.VMEM((2, 1, LANES), F32), pltpu.VMEM((2, 256, 1, LANES), F32),
            dma((3,)), dma((2,)), dma((NB,)), dma((NC,)),
            dma((10,)), dma((10,)), dma((4,)), dma((3,)), dma((4,)), dma((2,)),
        ],
        compiler_params=pltpu.CompilerParams(
            collective_id=0, has_side_effects=True, vmem_limit_bytes=60 * 2**20),
        name="conjugate",
    )(features, projection.T, targets.reshape(1, BLK))
    terms = terms.reshape(4, BLK)
    return terms[0] + terms[1], terms[2] - terms[3]


def solution(mesh):
    in_specs = (P(("wide", "narrow"), None), P(), P(("wide", "narrow")))
    out_specs = (P(("wide", "narrow")), P(("wide", "narrow")))
    return jax.shard_map(
        on_device, mesh=mesh, in_specs=in_specs, out_specs=out_specs, check_vma=False)
```
